512 devices in a mesh: seq: 64 (over x, y, z_hi), head: 8 (over z_lo, core).
Axes of the slice: x: 4, y: 8, z: 8 (z_hi: 2, z_lo: 4; z = z_hi * 4 + z_lo), core: 2. Of those that a mesh axis runs over, the one named last changes fastest.
Arguments:
- query: bfloat16 [8192, 64, 512], P('seq', 'head'), may hold values from -100 to 100
- latent: bfloat16 [8192, 512], P('seq'), may hold values from -6 to 6
- segment_ids: int32 [8192], replicated, may hold values from 0 to 31, never falling along the last dimension, each value on 1 to 3072 neighbouring positions
- block_of_slot: int32 [128], replicated, may hold values from 0 to 127, each once
- value_up: bfloat16 [64, 448, 128], P('head'), may hold values from -0.25 to 0.25
- out_proj: bfloat16 [8192, 3584], P('head', 'seq'), may hold values from -0.0625 to 0.0625
Outputs:
- mixed: bfloat16 [8192, 3584], P(('seq', 'head'))
The draws below stay inside these ranges and needn't reach their ends.
Inputs may be any that keep to these rules, and one draw needn't show every extreme that they name: segment_ids never falls along positions; every document has 1 to 3072 positions and one has exactly 3072. block_of_slot holds every position block once.
All inputs are finite; a program needn't handle non-finite values.
Results may differ from the reference program's by a relative error of at most 0.022.
Values may be sent and summed in bfloat16 or wider, within the bound.
No kernel may reach another device: no remote copies, remote signals or barrier semaphores. Data moves between devices by JAX's collectives and lax.ppermute only.
A program may use at most 64 MiB of HBM per device.

```python
import math
import jax
import jax.numpy as jnp
import numpy as np
from jax import lax

BLOCK = 64
H = 64
VH = 128
LATENT = 448
ROPE = 64
D = 3584
TOK_DEV = 128
TOKENS = 8192
DOC_MOST = 3072
DOCS = 32
N_SEQ = 64
N_HEAD = 8


def shared_latent(key):
    return jnp.clip(jax.random.normal(key, (TOKENS, LATENT + ROPE), jnp.float32), -6.0, 6.0)


def draw_latent(key, part):
    base = shared_latent(key)
    return base.astype(jnp.bfloat16)


def draw_query(key, part):
    key = jax.random.fold_in(key, 23)
    key_one = jax.random.fold_in(key, 0)
    shape = (TOKENS, H, LATENT + ROPE)
    values = 0.6 * jax.random.normal(key_one, shape, jnp.float32)
    return jnp.clip(values, -100.0, 100.0).astype(jnp.bfloat16)


def block_levels(key, extent, shards, smallest, top_value):
    def one(axis_at, shards_of):
        draws = jax.random.uniform(jax.random.fold_in(jax.random.fold_in(key, 6), axis_at), (shards_of,), jnp.float32, smallest / len(shards), top_value / len(shards))
        return jnp.repeat(jnp.exp(draws), extent[axis_at] // shards_of).reshape((-1,) + (1,) * (len(extent) - axis_at - 1))

    loudness = one(*shards[0])
    for cut in shards[1:]:
        loudness = loudness * one(*cut)
    return loudness


def split_up(number_of, total, bound, lean):
    loads = [(1 << 20) // math.isqrt(grade ** lean) + 1 for grade in range(2, number_of + 1)]
    rest, counts = total - bound - (number_of - 1), [1] * (number_of - 1)
    while rest > 0:
        candidates = [i for i in range(number_of - 1) if counts[i] < bound]
        pool, left = sum([loads[i] for i in candidates]), rest
        for i in candidates:
            extra = min(bound - counts[i], max(1, left * loads[i] // pool), rest)
            counts[i] = counts[i] + extra
            rest = rest - extra
    return np.array([bound] + counts)


def uneven(own_key, amount, total, most, lean):
    if amount == 2:
        one = jax.random.randint(own_key, (), max(1, total - most), min(most, total - 1) + 1)
        return jnp.stack([one, total - one])
    sizes = jnp.asarray(split_up(amount, total, most, lean), jnp.int32)
    couples = (amount - 1) // 2
    source_of, sink = sizes[1:1 + 2 * couples:2], sizes[2:2 + 2 * couples:2]
    room = jnp.minimum(source_of - 1, most - sink)
    moved = jax.random.randint(jax.random.fold_in(own_key, 1), (couples,), 0, 1 << 20) % (room + 1)
    sizes = sizes.at[1:1 + 2 * couples:2].set(source_of - moved).at[2:2 + 2 * couples:2].set(sink + moved)
    return sizes[jax.random.permutation(jax.random.fold_in(own_key, 2), amount)]


def gaussian(key, extent, scale, bound, shards=(), held_as=jnp.bfloat16):
    loudness = block_levels(key, extent, shards, -0.22, 0.18) if shards else 1.0
    array = jax.random.normal(key, extent, jnp.float32) * scale * loudness
    return jnp.minimum(jnp.maximum(array, -bound), bound).astype(held_as)


def setup_inputs(seed: int = 0) -> dict:
    streams_of = jax.random.split(jax.random.key(seed), 7)
    return {
        "query": draw_query(jax.random.fold_in(streams_of[6], 71), 0),
        "latent": draw_latent(jax.random.fold_in(streams_of[6], 71), 0),
        "segment_ids": jnp.searchsorted(jnp.cumsum(uneven(streams_of[2], DOCS, TOKENS, DOC_MOST, 2)), jnp.arange(TOKENS), side="right").astype(jnp.int32),
        "block_of_slot": jax.random.permutation(streams_of[3], 2 * N_SEQ).astype(jnp.int32),
        "value_up": gaussian(streams_of[4], (H, LATENT, VH), LATENT ** -0.5, 0.25, ((0, 8),)),
        "out_proj": gaussian(streams_of[5], (H * VH, D), (H * VH) ** -0.5, 0.0625, ((0, 8), (1, 64))),
    }


score_scale = 192 ** -0.5
negative = -1e30


def reference(query, latent, segment_ids, block_of_slot, value_up, out_proj):
    offsets = jnp.arange(BLOCK, dtype=jnp.int32)
    positions = (block_of_slot.astype(jnp.int32)[:, None] * BLOCK + offsets[None, :]).reshape(-1).astype(jnp.int32)
    segments = segment_ids.astype(jnp.int32)
    query_ord = jnp.zeros_like(query).at[positions].set(query)
    latent_ord = jnp.zeros_like(latent).at[positions].set(latent)
    padding = DOC_MOST
    latent_pad = jnp.concatenate([jnp.zeros((padding, LATENT + ROPE), latent.dtype), latent_ord], 0)
    seg_pad = jnp.concatenate([jnp.full((padding,), -1, jnp.int32), segments], 0)
    window = padding + TOK_DEV

    def one_block(number):
        start = (number * TOK_DEV).astype(jnp.int32)
        queries = lax.dynamic_slice_in_dim(query_ord, start, TOK_DEV, 0)
        key_rows = lax.dynamic_slice_in_dim(latent_pad, start, window, 0)
        key_seg = lax.dynamic_slice_in_dim(seg_pad, start, window, 0)
        query_seg = lax.dynamic_slice_in_dim(segments, start, TOK_DEV, 0)
        query_pos = start + jnp.arange(TOK_DEV, dtype=jnp.int32)
        key_pos = start - padding + jnp.arange(window, dtype=jnp.int32)
        allowed = (key_pos[None, :] <= query_pos[:, None]) & (key_seg[None, :] == query_seg[:, None])
        scores = jnp.einsum('qhc,kc->hqk', queries.astype(jnp.float32), key_rows.astype(jnp.float32)) * score_scale
        masked = jnp.where(allowed[None], scores, negative)
        maximum = jnp.max(masked, axis=-1, keepdims=True)
        weights = jnp.where(allowed[None], jnp.exp(masked - maximum), 0.0)
        total = jnp.sum(weights, axis=-1)
        weights_b = lax.optimization_barrier(weights.astype(jnp.bfloat16)).astype(jnp.float32)
        summed = jnp.einsum('hqk,kc->hqc', weights_b, key_rows[:, :LATENT].astype(jnp.float32))
        latent_out = (summed / total[..., None]).astype(jnp.bfloat16)
        head_values = jnp.einsum('hqc,hcv->qhv', latent_out.astype(jnp.float32), value_up.astype(jnp.float32))
        return head_values.astype(jnp.bfloat16)

    values_ord = lax.map(one_block, jnp.arange(N_SEQ, dtype=jnp.int32)).reshape(TOKENS, H, VH)
    values_slot = values_ord[positions]
    group_heads = H // N_HEAD
    summed_out = jnp.zeros((TOKENS, D), jnp.float32)
    for group in range(N_HEAD):
        group_values = values_slot[:, group * group_heads:(group + 1) * group_heads].reshape(TOKENS, group_heads * VH)
        group_rows = out_proj[group * group_heads * VH:(group + 1) * group_heads * VH]
        partial_value = jnp.dot(group_values, group_rows, preferred_element_type=jnp.float32).astype(jnp.bfloat16)
        summed_out = summed_out + lax.optimization_barrier(partial_value).astype(jnp.float32)
    return summed_out.astype(jnp.bfloat16)
```

```python
import functools
import math

import jax
import jax.numpy as jnp
from jax import lax
from jax.experimental import pallas as pl
from jax.experimental.pallas import tpu as pltpu
from jax.sharding import Mesh
from jax.sharding import PartitionSpec as P

BLK = 64
CHUNK = 8
KEYS = BLK * CHUNK
PART = 16
exp2_scale = 192 ** (-0.5) * math.log2(math.e)
floor_max = -1e30
masked_score = -2e30


def attention_kernel(n_pieces, part_stride, scal, lo_ref, q_ref, vup_ref, *rest):
    pieces = rest[:n_pieces]
    out_ref, lat, kbuf, acc, done, sems = rest[n_pieces:]
    heads, toks, width = q_ref.shape
    rows = heads * BLK
    copies = []
    at = 0
    for i, piece in enumerate(pieces):
        n = piece.shape[0]
        copies.append(pltpu.make_async_copy(piece, lat.at[pl.ds(at, n)], sems.at[i]))
        at += n
    for c in copies:
        c.start()
    for c in copies:
        c.wait()
    last_block = scal.shape[0] - 5

    for b in range(toks // BLK):
        block = scal[b]
        first = scal[2 + b]
        q = q_ref[:, b * BLK : (b + 1) * BLK, :].reshape(rows, width)
        lo = lo_ref[:, b * BLK : (b + 1) * BLK, :].reshape(rows, 1)
        pos = block * BLK + lax.broadcasted_iota(jnp.int32, (heads, BLK, 1), 1).reshape(rows, 1)
        acc[...] = jnp.zeros_like(acc)

        def step(i, carry):
            m, total = carry
            base = first + i * CHUNK
            for j in range(CHUNK):
                src = scal[4 + jnp.minimum(base + j, last_block)]
                for part in range(BLK // PART):
                    row = pl.multiple_of(src * PART + part * part_stride, PART)
                    at = j * BLK + part * PART
                    kbuf[at : at + PART, :] = lat[pl.ds(row, PART), :]
            keys = kbuf[...]
            s = lax.dot_general(q, keys, (((1,), (1,)), ((), ())), preferred_element_type=jnp.float32)
            kp = base * BLK + lax.broadcasted_iota(jnp.int32, (1, KEYS), 1)
            allowed = (kp <= pos) & (kp >= lo)
            s = jnp.where(allowed, s * exp2_scale, masked_score)
            new = jnp.maximum(m, jnp.max(s, axis=1, keepdims=True))
            w = jnp.exp2(s - new)
            factor = jnp.exp2(m - new)
            total = total * factor + jnp.sum(w, axis=1, keepdims=True)
            acc[...] = acc[...] * factor + jnp.dot(
                w.astype(jnp.bfloat16), keys, preferred_element_type=jnp.float32
            )
            return new, total

        count = (block - first + CHUNK) // CHUNK
        init = (jnp.full((rows, 1), floor_max, jnp.float32), jnp.zeros((rows, 1), jnp.float32))
        _, total = lax.fori_loop(0, count, step, init)
        latent_out = (acc[...] / total).astype(jnp.bfloat16)
        done[:, b * BLK : (b + 1) * BLK, :] = latent_out.reshape(heads, BLK, width)

    vh = vup_ref.shape[2]
    for h in range(heads):
        out_ref[:, h * vh : (h + 1) * vh] = jnp.dot(
            done[h], vup_ref[h], preferred_element_type=jnp.float32
        ).astype(jnp.bfloat16)


def attention(scal, lo, q, vup, pieces, part_stride):
    heads, toks, width = q.shape
    vh = vup.shape[2]
    total_rows = sum(p.shape[0] for p in pieces)
    vmem = pl.BlockSpec(memory_space=pltpu.VMEM)
    return pl.pallas_call(
        functools.partial(attention_kernel, len(pieces), part_stride),
        out_shape=jax.ShapeDtypeStruct((toks, heads * vh), jnp.bfloat16),
        in_specs=[pl.BlockSpec(memory_space=pltpu.SMEM), vmem, vmem, vmem]
        + [pl.BlockSpec(memory_space=pl.ANY)] * len(pieces),
        out_specs=vmem,
        scratch_shapes=[
            pltpu.VMEM((total_rows, width), jnp.bfloat16),
            pltpu.VMEM((KEYS, width), jnp.bfloat16),
            pltpu.VMEM((heads * BLK, width), jnp.float32),
            pltpu.VMEM((heads, toks, width), jnp.bfloat16),
            pltpu.SemaphoreType.DMA((len(pieces),)),
        ],
        compiler_params=pltpu.CompilerParams(vmem_limit_bytes=40 * 2**20),
        name="latent_attention",
    )(scal, lo, q, vup, *pieces)


def prepare(query, segment_ids, block_of_slot, value_up, seq_index):
    toks, heads, _ = query.shape
    my_blocks = lax.dynamic_slice_in_dim(block_of_slot, 2 * seq_index, 2, 0)
    segs = jnp.concatenate(
        [lax.dynamic_slice_in_dim(segment_ids, my_blocks[i] * BLK, BLK, 0) for i in range(2)]
    )
    lo = jnp.sum((segment_ids[None, :] < segs[:, None]).astype(jnp.int32), axis=1)
    first = lo.reshape(2, BLK)[:, 0] // BLK
    n = block_of_slot.shape[0]
    slots = jnp.arange(n, dtype=jnp.int32)
    slot_of_block = jnp.sum(
        jnp.where(block_of_slot[None, :] == slots[:, None], slots[None, :], 0), axis=1
    )
    lo_rows = jnp.broadcast_to(lo[None, :, None], (heads, toks, 1))
    q = query.transpose(1, 0, 2)
    vup = jnp.pad(value_up, ((0, 0), (0, query.shape[2] - value_up.shape[1]), (0, 0)))
    return my_blocks, first, slot_of_block, lo_rows, q, vup


def per_device(query, latent, segment_ids, block_of_slot, value_up, out_proj):
    nx, ny, nzh = (lax.axis_size(a) for a in ("x", "y", "zh"))
    nzl, nc = lax.axis_size("zl"), lax.axis_size("core")
    plane = nx * ny
    x, y, zh = (lax.axis_index(a) for a in ("x", "y", "zh"))
    zl, core = lax.axis_index("zl"), lax.axis_index("core")
    seq_index = (x * ny + y) * nzh + zh

    part = lax.dynamic_slice_in_dim(latent, (zl * nc + core) * PART, PART, 0)
    spread = jnp.broadcast_to(part[None], (plane,) + part.shape)
    plane_rows = lax.all_to_all(spread, ("x", "y"), 0, 0, tiled=True)
    plane_rows = plane_rows.reshape(plane * PART, latent.shape[1])
    gathered = lax.all_gather(plane_rows, ("zh", "zl", "core"), axis=0, tiled=True)

    cols = out_proj.T
    other = lax.ppermute(cols, "zh", [(i, nzh - 1 - i) for i in range(nzh)])
    pair = jnp.where(zh == 0, jnp.stack([cols, other]), jnp.stack([other, cols]))
    columns = lax.all_gather(pair.reshape(-1, cols.shape[1]), "y", axis=0, tiled=True)

    my_blocks, first, slot_of_block, lo_rows, q, vup = prepare(
        query, segment_ids, block_of_slot, value_up, seq_index
    )
    slot_seq, slot_half = slot_of_block // 2, slot_of_block % 2
    parts = BLK // PART
    start = ((slot_seq % nzh) * 2 * parts + slot_half * parts) * plane + slot_seq // nzh
    scal = jnp.concatenate([my_blocks, first, start]).astype(jnp.int32)
    head_values = attention(scal, lo_rows, q, vup, [gathered], plane * PART)

    toks, wide = head_values.shape
    spread = jnp.broadcast_to(head_values[None], (nx, toks, wide))
    rows = lax.all_to_all(spread, "x", 0, 0, tiled=True).reshape(nx * toks, wide)
    partial_value = lax.dot_general(
        rows, columns, (((1,), (1,)), ((), ())), preferred_element_type=jnp.float32
    ).astype(jnp.bfloat16)
    n_cols = columns.shape[0]
    own = toks // (nzl * nc)
    partial_value = partial_value.reshape(nx * nzl, nc, own, n_cols)
    keep = lax.dynamic_index_in_dim(partial_value, core, 1, keepdims=False)
    give = lax.dynamic_index_in_dim(partial_value, nc - 1 - core, 1, keepdims=False)
    got = lax.ppermute(give, "core", [(i, nc - 1 - i) for i in range(nc)])
    chip = (keep.astype(jnp.float32) + got.astype(jnp.float32)).astype(jnp.bfloat16)
    terms = lax.all_to_all(chip, ("x", "zl"), 0, 0, tiled=True)
    terms = terms.reshape(nx, nzl, own, n_cols).astype(jnp.float32)
    mixed = jnp.sum(terms, axis=1).astype(jnp.bfloat16)
    return mixed.transpose(1, 0, 2).reshape(own, nx * n_cols)


AXES = {"x": 4, "y": 8, "zh": 2, "zl": 4, "core": 2}


def solution(mesh):
    names = tuple(AXES)
    fine = Mesh(mesh.devices.reshape(tuple(AXES.values())), names)
    seq, head = names[:3], names[3:]
    return jax.shard_map(
        per_device,
        mesh=fine,
        in_specs=(
            P(seq, head, None),
            P(seq, None),
            P(),
            P(),
            P(head, None, None),
            P(head, seq),
        ),
        out_specs=P(names, None),
        check_vma=False,
    )
```

```python
import functools
import math

import jax
import jax.numpy as jnp
from jax import lax
from jax.experimental import pallas as pl
from jax.experimental.pallas import tpu as pltpu
from jax.sharding import Mesh
from jax.sharding import PartitionSpec as P

BLK = 64
CHUNK = 8
KEYS = BLK * CHUNK
ROWS, LANES = 32, 128
PARTS = 8
exp2_scale = 192 ** (-0.5) * math.log2(math.e)
floor_max = -1e30
masked_score = -2e30


def attention_kernel(scal, lo_ref, q_ref, vup_ref, lat, out_ref, kbuf, acc, done):
    heads, toks, width = q_ref.shape
    rows = heads * BLK
    slices = lat.shape[0] // 16
    across = width // LANES
    last_block = scal.shape[0] - 5

    for b in range(toks // BLK):
        block = scal[b]
        first = scal[2 + b]
        q = q_ref[:, b * BLK : (b + 1) * BLK, :].reshape(rows, width)
        lo = lo_ref[:, b * BLK : (b + 1) * BLK, :].reshape(rows, 1)
        pos = block * BLK + lax.broadcasted_iota(jnp.int32, (heads, BLK, 1), 1).reshape(rows, 1)
        acc[...] = jnp.zeros_like(acc)

        def step(i, carry):
            m, total = carry
            base = first + i * CHUNK
            for j in range(CHUNK):
                src = scal[4 + jnp.minimum(base + j, last_block)]
                for part in range(PARTS):
                    row = j * BLK + part // across * ROWS
                    lane = part % across * LANES
                    kbuf[row : row + ROWS, lane : lane + LANES] = lat[src + part * slices]
            keys = kbuf[...]
            s = lax.dot_general(q, keys, (((1,), (1,)), ((), ())), preferred_element_type=jnp.float32)
            kp = base * BLK + lax.broadcasted_iota(jnp.int32, (1, KEYS), 1)
            allowed = (kp <= pos) & (kp >= lo)
            s = jnp.where(allowed, s * exp2_scale, masked_score)
            new = jnp.maximum(m, jnp.max(s, axis=1, keepdims=True))
            w = jnp.exp2(s - new)
            factor = jnp.exp2(m - new)
            total = total * factor + jnp.sum(w, axis=1, keepdims=True)
            acc[...] = acc[...] * factor + jnp.dot(
                w.astype(jnp.bfloat16), keys, preferred_element_type=jnp.float32
            )
            return new, total

        count = (block - first + CHUNK) // CHUNK
        init = (jnp.full((rows, 1), floor_max, jnp.float32), jnp.zeros((rows, 1), jnp.float32))
        _, total = lax.fori_loop(0, count, step, init)
        latent_out = (acc[...] / total).astype(jnp.bfloat16)
        done[:, b * BLK : (b + 1) * BLK, :] = latent_out.reshape(heads, BLK, width)

    vh = vup_ref.shape[2]
    for h in range(heads):
        out_ref[:, h * vh : (h + 1) * vh] = jnp.dot(
            done[h], vup_ref[h], preferred_element_type=jnp.float32
        ).astype(jnp.bfloat16)


def attention(scal, lo, q, vup, lat):
    heads, toks, width = q.shape
    vh = vup.shape[2]
    vmem = pl.BlockSpec(memory_space=pltpu.VMEM)
    return pl.pallas_call(
        attention_kernel,
        out_shape=jax.ShapeDtypeStruct((toks, heads * vh), jnp.bfloat16),
        in_specs=[pl.BlockSpec(memory_space=pltpu.SMEM)] + [vmem] * 4,
        out_specs=vmem,
        scratch_shapes=[
            pltpu.VMEM((KEYS, width), jnp.bfloat16),
            pltpu.VMEM((heads * BLK, width), jnp.float32),
            pltpu.VMEM((heads, toks, width), jnp.bfloat16),
        ],
        compiler_params=pltpu.CompilerParams(vmem_limit_bytes=40 * 2**20),
        name="latent_attention",
    )(scal, lo, q, vup, lat)


def prepare(query, segment_ids, block_of_slot, value_up, seq_index):
    toks, heads, _ = query.shape
    my_blocks = lax.dynamic_slice_in_dim(block_of_slot, 2 * seq_index, 2, 0)
    segs = jnp.concatenate(
        [lax.dynamic_slice_in_dim(segment_ids, my_blocks[i] * BLK, BLK, 0) for i in range(2)]
    )
    lo = jnp.sum((segment_ids[None, :] < segs[:, None]).astype(jnp.int32), axis=1)
    first = lo.reshape(2, BLK)[:, 0] // BLK
    n = block_of_slot.shape[0]
    slots = jnp.arange(n, dtype=jnp.int32)
    slot_of_block = jnp.sum(
        jnp.where(block_of_slot[None, :] == slots[:, None], slots[None, :], 0), axis=1
    )
    lo_rows = jnp.broadcast_to(lo[None, :, None], (heads, toks, 1))
    q = query.transpose(1, 0, 2)
    vup = jnp.pad(value_up, ((0, 0), (0, query.shape[2] - value_up.shape[1]), (0, 0)))
    return my_blocks, first, slot_of_block, lo_rows, q, vup


def per_device(query, latent, segment_ids, block_of_slot, value_up, out_proj):
    nx, ny, nzh = (lax.axis_size(a) for a in ("x", "y", "zh"))
    nzl, nc = lax.axis_size("zl"), lax.axis_size("core")
    plane = nx * ny
    x, y, zh = (lax.axis_index(a) for a in ("x", "y", "zh"))
    zl, core = lax.axis_index("zl"), lax.axis_index("core")
    seq_index = (x * ny + y) * nzh + zh
    toks, width = latent.shape
    halves, across = toks // BLK, width // LANES

    part = latent.reshape(halves, BLK // ROWS, ROWS, across, LANES).transpose(1, 3, 0, 2, 4)
    part = part.reshape(PARTS, halves, ROWS, LANES)
    part = lax.dynamic_index_in_dim(part, zl * nc + core, 0, keepdims=False)
    spread = jnp.broadcast_to(part[None], (plane,) + part.shape)
    plane_rows = lax.all_to_all(spread, ("x", "y"), 0, 0, tiled=True)
    out_proj, plane_rows = lax.optimization_barrier((out_proj, plane_rows))
    gathered = lax.all_gather(
        plane_rows.reshape(plane * halves * ROWS, LANES), ("zh", "zl", "core"), axis=0, tiled=True
    )
    gathered = gathered.reshape(-1, ROWS, LANES)

    cols = out_proj.T
    other = lax.ppermute(cols, "zh", [(i, nzh - 1 - i) for i in range(nzh)])

    def over_y(piece):
        return lax.all_to_all(jnp.broadcast_to(piece[None], (ny,) + piece.shape), "y", 0, 0, tiled=True)

    mine = over_y(cols)
    theirs = over_y(other)
    columns = jnp.where(zh == 0, jnp.stack([mine, theirs], 1), jnp.stack([theirs, mine], 1))
    columns = columns.reshape(-1, cols.shape[1])

    my_blocks, first, slot_of_block, lo_rows, q, vup = prepare(
        query, segment_ids, block_of_slot, value_up, seq_index
    )
    slot_seq, slot_half = slot_of_block // 2, slot_of_block % 2
    slices = plane * halves
    start = (slot_seq % nzh) * PARTS * slices + slot_seq // nzh * halves + slot_half
    scal = jnp.concatenate([my_blocks, first, start]).astype(jnp.int32)
    scal, columns = lax.optimization_barrier((scal, columns))
    head_values = attention(scal, lo_rows, q, vup, gathered)

    wide = head_values.shape[1]
    spread = jnp.broadcast_to(head_values[None], (nx, toks, wide))
    rows = lax.all_to_all(spread, "x", 0, 0, tiled=True).reshape(nx * toks, wide)
    partial_value = lax.dot_general(
        rows, columns, (((1,), (1,)), ((), ())), preferred_element_type=jnp.float32
    ).astype(jnp.bfloat16)
    n_cols = columns.shape[0]
    own = toks // (nzl * nc)
    partial_value = partial_value.reshape(nx * nzl, nc, own, n_cols)
    keep = lax.dynamic_index_in_dim(partial_value, core, 1, keepdims=False)
    give = lax.dynamic_index_in_dim(partial_value, nc - 1 - core, 1, keepdims=False)
    got = lax.ppermute(give, "core", [(i, nc - 1 - i) for i in range(nc)])
    chip = (keep.astype(jnp.float32) + got.astype(jnp.float32)).astype(jnp.bfloat16)
    terms = lax.all_to_all(chip, ("x", "zl"), 0, 0, tiled=True)
    terms = terms.reshape(nx, nzl, own, n_cols).astype(jnp.float32)
    mixed = jnp.sum(terms, axis=1).astype(jnp.bfloat16)
    return mixed.transpose(1, 0, 2).reshape(own, nx * n_cols)


AXES = {"x": 4, "y": 8, "zh": 2, "zl": 4, "core": 2}


def solution(mesh):
    names = tuple(AXES)
    fine = Mesh(mesh.devices.reshape(tuple(AXES.values())), names)
    seq, head = names[:3], names[3:]
    return jax.shard_map(
        per_device,
        mesh=fine,
        in_specs=(
            P(seq, head, None),
            P(seq, None),
            P(),
            P(),
            P(head, None, None),
            P(head, seq),
        ),
        out_specs=P(names, None),
        check_vma=False,
    )
```

```python
import functools
import math

import jax
import jax.numpy as jnp
from jax import lax
from jax.experimental import pallas as pl
from jax.experimental.pallas import tpu as pltpu
from jax.sharding import Mesh
from jax.sharding import PartitionSpec as P

BLK = 64
CHUNK = 8
KEYS = BLK * CHUNK
ROWS, LANES = 32, 128
PARTS = 8
FEW = 44
exp2_scale = 192 ** (-0.5) * math.log2(math.e)
floor_max = -1e30
masked_score = -2e30


def attention_kernel(scal, lo_ref, q_ref, vup_ref, lat, out_ref, kbuf, acc, done):
    heads, toks, width = q_ref.shape
    rows = heads * BLK
    slices = lat.shape[0] // 16
    across = width // LANES
    last_block = scal.shape[0] - 5

    for b in range(toks // BLK):
        block = scal[b]
        first = scal[2 + b]
        q = q_ref[:, b * BLK : (b + 1) * BLK, :].reshape(rows, width)
        lo = lo_ref[:, b * BLK : (b + 1) * BLK, :].reshape(rows, 1)
        pos = block * BLK + lax.broadcasted_iota(jnp.int32, (heads, BLK, 1), 1).reshape(rows, 1)
        acc[...] = jnp.zeros_like(acc)

        def step(i, carry):
            m, total = carry
            base = first + i * CHUNK
            for j in range(CHUNK):
                src = scal[4 + jnp.minimum(base + j, last_block)]
                for part in range(PARTS):
                    row = j * BLK + part // across * ROWS
                    lane = part % across * LANES
                    kbuf[row : row + ROWS, lane : lane + LANES] = lat[src + part * slices]
            keys = kbuf[...]
            s = lax.dot_general(q, keys, (((1,), (1,)), ((), ())), preferred_element_type=jnp.float32)
            kp = base * BLK + lax.broadcasted_iota(jnp.int32, (1, KEYS), 1)
            allowed = (kp <= pos) & (kp >= lo)
            s = jnp.where(allowed, s * exp2_scale, masked_score)
            new = jnp.maximum(m, jnp.max(s, axis=1, keepdims=True))
            w = jnp.exp2(s - new)
            factor = jnp.exp2(m - new)
            total = total * factor + jnp.sum(w, axis=1, keepdims=True)
            acc[...] = acc[...] * factor + jnp.dot(
                w.astype(jnp.bfloat16), keys, preferred_element_type=jnp.float32
            )
            return new, total

        count = (block - first + CHUNK) // CHUNK
        init = (jnp.full((rows, 1), floor_max, jnp.float32), jnp.zeros((rows, 1), jnp.float32))
        _, total = lax.fori_loop(0, count, step, init)
        latent_out = (acc[...] / total).astype(jnp.bfloat16)
        done[:, b * BLK : (b + 1) * BLK, :] = latent_out.reshape(heads, BLK, width)

    vh = vup_ref.shape[2]
    for h in range(heads):
        out_ref[:, h * vh : (h + 1) * vh] = jnp.dot(
            done[h], vup_ref[h], preferred_element_type=jnp.float32
        ).astype(jnp.bfloat16)


def attention(scal, lo, q, vup, lat):
    heads, toks, width = q.shape
    vh = vup.shape[2]
    vmem = pl.BlockSpec(memory_space=pltpu.VMEM)
    return pl.pallas_call(
        attention_kernel,
        out_shape=jax.ShapeDtypeStruct((toks, heads * vh), jnp.bfloat16),
        in_specs=[pl.BlockSpec(memory_space=pltpu.SMEM)] + [vmem] * 4,
        out_specs=vmem,
        scratch_shapes=[
            pltpu.VMEM((KEYS, width), jnp.bfloat16),
            pltpu.VMEM((heads * BLK, width), jnp.float32),
            pltpu.VMEM((heads, toks, width), jnp.bfloat16),
        ],
        compiler_params=pltpu.CompilerParams(vmem_limit_bytes=40 * 2**20),
        name="latent_attention",
    )(scal, lo, q, vup, lat)


def prepare(query, segment_ids, block_of_slot, value_up, seq_index):
    toks, heads, _ = query.shape
    my_blocks = lax.dynamic_slice_in_dim(block_of_slot, 2 * seq_index, 2, 0)
    segs = jnp.concatenate(
        [lax.dynamic_slice_in_dim(segment_ids, my_blocks[i] * BLK, BLK, 0) for i in range(2)]
    )
    lo = jnp.sum((segment_ids[None, :] < segs[:, None]).astype(jnp.int32), axis=1)
    first = lo.reshape(2, BLK)[:, 0] // BLK
    n = block_of_slot.shape[0]
    slots = jnp.arange(n, dtype=jnp.int32)
    slot_of_block = jnp.sum(
        jnp.where(block_of_slot[None, :] == slots[:, None], slots[None, :], 0), axis=1
    )
    lo_rows = jnp.broadcast_to(lo[None, :, None], (heads, toks, 1))
    q = query.transpose(1, 0, 2)
    vup = jnp.pad(value_up, ((0, 0), (0, query.shape[2] - value_up.shape[1]), (0, 0)))
    return my_blocks, first, slot_of_block, lo_rows, q, vup


def need_tables(segment_ids, block_of_slot, plane, nzh, halves):
    n = block_of_slot.shape[0]
    firsts = segment_ids.reshape(n, BLK)[:, 0]
    block_first = jnp.sum((segment_ids[None, :] < firsts[:, None]).astype(jnp.int32), axis=1) // BLK
    blocks = jnp.arange(n, dtype=jnp.int32)
    slot_first = jnp.sum(
        jnp.where(block_of_slot[:, None] == blocks[None, :], block_first[None, :], 0), axis=1
    )
    pair = (slot_first[:, None] <= block_of_slot[None, :]) & (
        block_of_slot[None, :] <= block_of_slot[:, None]
    )
    need = jnp.any(pair.reshape(plane, nzh * halves, n), axis=1)
    slot_plane = blocks // halves % nzh
    before = (blocks[:, None] < blocks[None, :]) & (slot_plane[:, None] == slot_plane[None, :])
    rank = jnp.dot(need.astype(jnp.bfloat16), before.astype(jnp.bfloat16), preferred_element_type=jnp.float32)
    most = jnp.max(jnp.where(need, rank, -1.0)) + 1.0
    return need, rank, most <= FEW


def per_device(query, latent, segment_ids, block_of_slot, value_up, out_proj):
    nx, ny, nzh = (lax.axis_size(a) for a in ("x", "y", "zh"))
    nzl, nc = lax.axis_size("zl"), lax.axis_size("core")
    plane = nx * ny
    x, y, zh = (lax.axis_index(a) for a in ("x", "y", "zh"))
    zl, core = lax.axis_index("zl"), lax.axis_index("core")
    seq_index = (x * ny + y) * nzh + zh
    toks, width = latent.shape
    halves, across = toks // BLK, width // LANES
    slices = plane * halves

    cols = out_proj.T
    other = lax.ppermute(cols, "zh", [(i, nzh - 1 - i) for i in range(nzh)])

    part = latent.reshape(halves, BLK // ROWS, ROWS, across, LANES).transpose(1, 3, 0, 2, 4)
    part = part.reshape(PARTS, halves, ROWS, LANES)
    part = lax.dynamic_index_in_dim(part, zl * nc + core, 0, keepdims=False)
    spread = jnp.broadcast_to(part[None], (plane,) + part.shape)
    plane_rows = lax.all_to_all(spread, ("x", "y"), 0, 0, tiled=True)
    plane_rows = plane_rows.reshape(slices, ROWS * LANES)

    need, rank, fits = need_tables(segment_ids, block_of_slot, plane, nzh, halves)
    my_need = lax.dynamic_index_in_dim(need, x * ny + y, 0, keepdims=False)
    my_rank = lax.dynamic_index_in_dim(rank, x * ny + y, 0, keepdims=False).astype(jnp.int32)
    row_need = lax.dynamic_index_in_dim(my_need.reshape(plane, nzh, halves), zh, 1, keepdims=False)
    row_rank = lax.dynamic_index_in_dim(my_rank.reshape(plane, nzh, halves), zh, 1, keepdims=False)
    row_rank = jnp.where(row_need, row_rank, -1).reshape(1, slices)

    def over_y(piece):
        return lax.all_to_all(jnp.broadcast_to(piece[None], (ny,) + piece.shape), "y", 0, 0, tiled=True)

    def attend(few, operands):
        plane_rows, cols, other, query, segment_ids, block_of_slot, value_up, my_rank, row_rank = operands
        if few:
            kept = FEW
            pick = (row_rank == jnp.arange(kept, dtype=jnp.int32)[:, None]).astype(jnp.bfloat16)
            sent = jnp.dot(pick, plane_rows, preferred_element_type=jnp.float32).astype(jnp.bfloat16)
        else:
            kept = slices
            sent = plane_rows
        gathered = lax.all_gather(sent.reshape(kept * ROWS, LANES), ("zh", "zl", "core"), axis=0, tiled=True)
        gathered = gathered.reshape(-1, ROWS, LANES)

        cols, other, sent = lax.optimization_barrier((cols, other, sent))
        mine = over_y(cols)
        theirs = over_y(other)
        columns = jnp.where(zh == 0, jnp.stack([mine, theirs], 1), jnp.stack([theirs, mine], 1))
        columns = columns.reshape(-1, cols.shape[1])

        my_blocks, first, slot_of_block, lo_rows, q, vup = prepare(
            query, segment_ids, block_of_slot, value_up, seq_index
        )
        slot_seq, slot_half = slot_of_block // halves, slot_of_block % halves
        if few:
            slots = jnp.arange(block_of_slot.shape[0], dtype=jnp.int32)
            place = jnp.sum(jnp.where(slot_of_block[:, None] == slots[None, :], my_rank[None, :], 0), axis=1)
            place = jnp.minimum(place, kept - 1)
        else:
            place = slot_seq // nzh * halves + slot_half
        start = (slot_seq % nzh) * PARTS * kept + place
        scal = jnp.concatenate([my_blocks, first, start]).astype(jnp.int32)
        scal, columns = lax.optimization_barrier((scal, columns))
        return attention(scal, lo_rows, q, vup, gathered), columns

    head_values, columns = lax.cond(
        fits,
        functools.partial(attend, True),
        functools.partial(attend, False),
        (plane_rows, cols, other, query, segment_ids, block_of_slot, value_up, my_rank, row_rank),
    )

    wide = head_values.shape[1]
    spread = jnp.broadcast_to(head_values[None], (nx, toks, wide))
    rows = lax.all_to_all(spread, "x", 0, 0, tiled=True).reshape(nx * toks, wide)
    partial_value = lax.dot_general(
        rows, columns, (((1,), (1,)), ((), ())), preferred_element_type=jnp.float32
    ).astype(jnp.bfloat16)
    n_cols = columns.shape[0]
    own = toks // (nzl * nc)
    partial_value = partial_value.reshape(nx * nzl, nc, own, n_cols)
    keep = lax.dynamic_index_in_dim(partial_value, core, 1, keepdims=False)
    give = lax.dynamic_index_in_dim(partial_value, nc - 1 - core, 1, keepdims=False)
    got = lax.ppermute(give, "core", [(i, nc - 1 - i) for i in range(nc)])
    chip = (keep.astype(jnp.float32) + got.astype(jnp.float32)).astype(jnp.bfloat16)
    terms = lax.all_to_all(chip, ("x", "zl"), 0, 0, tiled=True)
    terms = terms.reshape(nx, nzl, own, n_cols).astype(jnp.float32)
    mixed = jnp.sum(terms, axis=1).astype(jnp.bfloat16)
    return mixed.transpose(1, 0, 2).reshape(own, nx * n_cols)


AXES = {"x": 4, "y": 8, "zh": 2, "zl": 4, "core": 2}


def solution(mesh):
    names = tuple(AXES)
    fine = Mesh(mesh.devices.reshape(tuple(AXES.values())), names)
    seq, head = names[:3], names[3:]
    return jax.shard_map(
        per_device,
        mesh=fine,
        in_specs=(
            P(seq, head, None),
            P(seq, None),
            P(),
            P(),
            P(head, None, None),
            P(head, seq),
        ),
        out_specs=P(names, None),
        check_vma=False,
    )
```

```python
import functools
import math

import jax
import jax.numpy as jnp
from jax import lax
from jax.experimental import pallas as pl
from jax.experimental.pallas import tpu as pltpu
from jax.sharding import Mesh
from jax.sharding import PartitionSpec as P

BLK = 64
CHUNK = 8
KEYS = BLK * CHUNK
ROWS, LANES = 32, 128
PARTS = 8
FEW = 44
exp2_scale = 192 ** (-0.5) * math.log2(math.e)
floor_max = -1e30
masked_score = -2e30


def attention_kernel(scal, lo_ref, q_ref, vup_ref, lat, out_ref, kbuf, acc, done):
    heads, toks, width = q_ref.shape
    rows = heads * BLK
    slices = lat.shape[0] // 16
    across = width // LANES
    last_block = scal.shape[0] - 5

    for b in range(toks // BLK):
        block = scal[b]
        first = scal[2 + b]
        q = q_ref[:, b * BLK : (b + 1) * BLK, :].reshape(rows, width)
        lo = lo_ref[:, b * BLK : (b + 1) * BLK, :].reshape(rows, 1)
        pos = block * BLK + lax.broadcasted_iota(jnp.int32, (heads, BLK, 1), 1).reshape(rows, 1)
        acc[...] = jnp.zeros_like(acc)

        def step(i, carry):
            m, total = carry
            base = first + i * CHUNK
            for j in range(CHUNK):
                src = scal[4 + jnp.minimum(base + j, last_block)]
                for part in range(PARTS):
                    row = j * BLK + part // across * ROWS
                    lane = part % across * LANES
                    kbuf[row : row + ROWS, lane : lane + LANES] = lat[src + part * slices]
            keys = kbuf[...]
            s = lax.dot_general(q, keys, (((1,), (1,)), ((), ())), preferred_element_type=jnp.float32)
            kp = base * BLK + lax.broadcasted_iota(jnp.int32, (1, KEYS), 1)
            allowed = (kp <= pos) & (kp >= lo)
            s = jnp.where(allowed, s * exp2_scale, masked_score)
            new = jnp.maximum(m, jnp.max(s, axis=1, keepdims=True))
            w = jnp.exp2(s - new)
            factor = jnp.exp2(m - new)
            total = total * factor + jnp.sum(w, axis=1, keepdims=True)
            acc[...] = acc[...] * factor + jnp.dot(
                w.astype(jnp.bfloat16), keys, preferred_element_type=jnp.float32
            )
            return new, total

        count = (block - first + CHUNK) // CHUNK
        init = (jnp.full((rows, 1), floor_max, jnp.float32), jnp.zeros((rows, 1), jnp.float32))
        _, total = lax.fori_loop(0, count, step, init)
        latent_out = (acc[...] / total).astype(jnp.bfloat16)
        done[:, b * BLK : (b + 1) * BLK, :] = latent_out.reshape(heads, BLK, width)

    vh = vup_ref.shape[2]
    for h in range(heads):
        values = jnp.dot(done[h], vup_ref[h], preferred_element_type=jnp.float32).astype(jnp.bfloat16)
        for copy in range(out_ref.shape[0]):
            out_ref[copy, :, h * vh : (h + 1) * vh] = values


def attention(scal, lo, q, vup, lat, copies):
    heads, toks, width = q.shape
    vh = vup.shape[2]
    vmem = pl.BlockSpec(memory_space=pltpu.VMEM)
    return pl.pallas_call(
        attention_kernel,
        out_shape=jax.ShapeDtypeStruct((copies, toks, heads * vh), jnp.bfloat16),
        in_specs=[pl.BlockSpec(memory_space=pltpu.SMEM)] + [vmem] * 4,
        out_specs=vmem,
        scratch_shapes=[
            pltpu.VMEM((KEYS, width), jnp.bfloat16),
            pltpu.VMEM((heads * BLK, width), jnp.float32),
            pltpu.VMEM((heads, toks, width), jnp.bfloat16),
        ],
        compiler_params=pltpu.CompilerParams(vmem_limit_bytes=40 * 2**20),
        cost_estimate=pl.CostEstimate(
            flops=6 * 2**30, bytes_accessed=2 * lat.size, transcendentals=2**21
        ),
        name="latent_attention",
    )(scal, lo, q, vup, lat)


def prepare(query, segment_ids, block_of_slot, value_up, seq_index):
    toks, heads, _ = query.shape
    my_blocks = lax.dynamic_slice_in_dim(block_of_slot, 2 * seq_index, 2, 0)
    segs = jnp.concatenate(
        [lax.dynamic_slice_in_dim(segment_ids, my_blocks[i] * BLK, BLK, 0) for i in range(2)]
    )
    lo = jnp.sum((segment_ids[None, :] < segs[:, None]).astype(jnp.int32), axis=1)
    first = lo.reshape(2, BLK)[:, 0] // BLK
    n = block_of_slot.shape[0]
    slots = jnp.arange(n, dtype=jnp.int32)
    slot_of_block = jnp.sum(
        jnp.where(block_of_slot[None, :] == slots[:, None], slots[None, :], 0), axis=1
    )
    lo_rows = jnp.broadcast_to(lo[None, :, None], (heads, toks, 1))
    q = query.transpose(1, 0, 2)
    vup = jnp.pad(value_up, ((0, 0), (0, query.shape[2] - value_up.shape[1]), (0, 0)))
    return my_blocks, first, slot_of_block, lo_rows, q, vup


def need_tables(segment_ids, block_of_slot, plane, nzh, halves):
    n = block_of_slot.shape[0]
    firsts = segment_ids.reshape(n, BLK)[:, 0]
    block_first = jnp.sum((segment_ids[None, :] < firsts[:, None]).astype(jnp.int32), axis=1) // BLK
    blocks = jnp.arange(n, dtype=jnp.int32)
    slot_first = jnp.sum(
        jnp.where(block_of_slot[:, None] == blocks[None, :], block_first[None, :], 0), axis=1
    )
    pair = (slot_first[:, None] <= block_of_slot[None, :]) & (
        block_of_slot[None, :] <= block_of_slot[:, None]
    )
    need = jnp.any(pair.reshape(plane, nzh * halves, n), axis=1)
    slot_plane = blocks // halves % nzh
    before = (blocks[:, None] < blocks[None, :]) & (slot_plane[:, None] == slot_plane[None, :])
    rank = jnp.dot(need.astype(jnp.bfloat16), before.astype(jnp.bfloat16), preferred_element_type=jnp.float32)
    most = jnp.max(jnp.where(need, rank, -1.0)) + 1.0
    return need, rank, most <= FEW


def per_device(query, latent, segment_ids, block_of_slot, value_up, out_proj):
    nx, ny, nzh = (lax.axis_size(a) for a in ("x", "y", "zh"))
    nzl, nc = lax.axis_size("zl"), lax.axis_size("core")
    plane = nx * ny
    x, y, zh = (lax.axis_index(a) for a in ("x", "y", "zh"))
    zl, core = lax.axis_index("zl"), lax.axis_index("core")
    seq_index = (x * ny + y) * nzh + zh
    toks, width = latent.shape
    halves, across = toks // BLK, width // LANES
    slices = plane * halves

    cols = out_proj.T
    other = lax.ppermute(cols, "zh", [(i, nzh - 1 - i) for i in range(nzh)])

    number = zl * nc + core
    corner = (0, number // across * ROWS, number % across * LANES)
    part = lax.dynamic_slice(latent.reshape(halves, BLK, width), corner, (halves, ROWS, LANES))
    spread = jnp.broadcast_to(part[None], (plane,) + part.shape)
    plane_rows = lax.all_to_all(spread, ("x", "y"), 0, 0, tiled=True)
    plane_rows = plane_rows.reshape(slices, ROWS * LANES)

    need, rank, fits = need_tables(segment_ids, block_of_slot, plane, nzh, halves)
    my_need = lax.dynamic_index_in_dim(need, x * ny + y, 0, keepdims=False)
    my_rank = lax.dynamic_index_in_dim(rank, x * ny + y, 0, keepdims=False).astype(jnp.int32)
    row_need = lax.dynamic_index_in_dim(my_need.reshape(plane, nzh, halves), zh, 1, keepdims=False)
    row_rank = lax.dynamic_index_in_dim(my_rank.reshape(plane, nzh, halves), zh, 1, keepdims=False)
    row_rank = jnp.where(row_need, row_rank, -1).reshape(1, slices)
    pick = (row_rank == jnp.arange(FEW, dtype=jnp.int32)[:, None]).astype(jnp.bfloat16)
    pick, my_rank = lax.optimization_barrier((pick, my_rank))

    def over_y(piece):
        return lax.all_to_all(jnp.broadcast_to(piece[None], (ny,) + piece.shape), "y", 0, 0, tiled=True)

    def attend(few, operands):
        plane_rows, cols, other, query, segment_ids, block_of_slot, value_up, my_rank, pick = operands
        if few:
            kept = FEW
            sent = jnp.dot(pick, plane_rows, preferred_element_type=jnp.float32).astype(jnp.bfloat16)
        else:
            kept = slices
            sent = plane_rows
        gathered = lax.all_gather(sent.reshape(kept * ROWS, LANES), ("zh", "zl", "core"), axis=0, tiled=True)
        gathered = gathered.reshape(-1, ROWS, LANES)

        cols, other, sent = lax.optimization_barrier((cols, other, sent))
        mine = over_y(cols)
        theirs = over_y(other)

        my_blocks, first, slot_of_block, lo_rows, q, vup = prepare(
            query, segment_ids, block_of_slot, value_up, seq_index
        )
        slot_seq, slot_half = slot_of_block // halves, slot_of_block % halves
        if few:
            slots = jnp.arange(block_of_slot.shape[0], dtype=jnp.int32)
            place = jnp.sum(jnp.where(slot_of_block[:, None] == slots[None, :], my_rank[None, :], 0), axis=1)
            place = jnp.minimum(place, kept - 1)
        else:
            place = slot_seq // nzh * halves + slot_half
        start = (slot_seq % nzh) * PARTS * kept + place
        scal = jnp.concatenate([my_blocks, first, start]).astype(jnp.int32)
        return attention(scal, lo_rows, q, vup, gathered, nx), mine, theirs

    head_values, mine, theirs = lax.cond(
        fits,
        functools.partial(attend, True),
        functools.partial(attend, False),
        (plane_rows, cols, other, query, segment_ids, block_of_slot, value_up, my_rank, pick),
    )

    wide = head_values.shape[2]
    rows = lax.all_to_all(head_values, "x", 0, 0, tiled=True).reshape(nx * toks, wide)
    columns = jnp.where(zh == 0, jnp.stack([mine, theirs], 1), jnp.stack([theirs, mine], 1))
    columns = columns.reshape(-1, cols.shape[1])
    partial_value = lax.dot_general(
        rows, columns, (((1,), (1,)), ((), ())), preferred_element_type=jnp.float32
    ).astype(jnp.bfloat16)
    n_cols = columns.shape[0]
    own = toks // (nzl * nc)
    partial_value = partial_value.reshape(nx * nzl, nc, own, n_cols)
    keep = lax.dynamic_index_in_dim(partial_value, core, 1, keepdims=False)
    give = lax.dynamic_index_in_dim(partial_value, nc - 1 - core, 1, keepdims=False)
    got = lax.ppermute(give, "core", [(i, nc - 1 - i) for i in range(nc)])
    chip = (keep.astype(jnp.float32) + got.astype(jnp.float32)).astype(jnp.bfloat16)
    terms = lax.all_to_all(chip, ("x", "zl"), 0, 0, tiled=True)
    terms = terms.reshape(nx, nzl, own, n_cols).astype(jnp.float32)
    mixed = jnp.sum(terms, axis=1).astype(jnp.bfloat16)
    return mixed.transpose(1, 0, 2).reshape(own, nx * n_cols)


AXES = {"x": 4, "y": 8, "zh": 2, "zl": 4, "core": 2}


def solution(mesh):
    names = tuple(AXES)
    fine = Mesh(mesh.devices.reshape(tuple(AXES.values())), names)
    seq, head = names[:3], names[3:]
    return jax.shard_map(
        per_device,
        mesh=fine,
        in_specs=(
            P(seq, head, None),
            P(seq, None),
            P(),
            P(),
            P(head, None, None),
            P(head, seq),
        ),
        out_specs=P(names, None),
        check_vma=False,
    )
```

```python
import functools
import math

import jax
import jax.numpy as jnp
from jax import lax
from jax.experimental import pallas as pl
from jax.experimental.pallas import tpu as pltpu
from jax.sharding import Mesh
from jax.sharding import PartitionSpec as P

BLK = 64
CHUNK = 8
ROWS, LANES = 32, 128
PARTS = 8
OWN = 16
FEW = 44
exp2_scale = 192 ** (-0.5) * math.log2(math.e)
floor_max = -1e30
masked_score = -2e30


def attention_kernel(scal, lo_ref, q_ref, vup_ref, lat, out_ref, kbuf, acc, top, mass, done):
    heads, toks, width = q_ref.shape
    rows = heads * BLK
    slices = lat.shape[0] // 16
    across = width // LANES
    n_blocks = scal.shape[0] - 6

    def attend(b, base, size, masked):
        for j in range(size):
            src = scal[6 + jnp.minimum(base + j, n_blocks - 1)]
            for part in range(PARTS):
                row = j * BLK + part // across * ROWS
                lane = part % across * LANES
                kbuf[row : row + ROWS, lane : lane + LANES] = lat[src + part * slices]
        keys = kbuf[: size * BLK, :]
        q = q_ref[:, b * BLK : (b + 1) * BLK, :].reshape(rows, width)
        s = lax.dot_general(q, keys, (((1,), (1,)), ((), ())), preferred_element_type=jnp.float32)
        if masked:
            lo = lo_ref[:, b * BLK : (b + 1) * BLK, :].reshape(rows, 1)
            pos = scal[b] * BLK + lax.broadcasted_iota(jnp.int32, (heads, BLK, 1), 1).reshape(rows, 1)
            kp = base * BLK + lax.broadcasted_iota(jnp.int32, (1, size * BLK), 1)
            s = jnp.where((kp <= pos) & (kp >= lo), s, masked_score)
        tiles = [s[:, t : t + LANES] for t in range(0, size * BLK, LANES)]
        old = top[...]
        new = jnp.maximum(old, jnp.max(functools.reduce(jnp.maximum, tiles), axis=1, keepdims=True))
        factor = jnp.exp2((old - new) * exp2_scale)
        w = [jnp.exp2((tile - new) * exp2_scale) for tile in tiles]
        top[...] = new
        mass[...] = mass[...] * factor + functools.reduce(jnp.add, w)
        added = jnp.dot(
            jnp.concatenate([x.astype(jnp.bfloat16) for x in w], axis=1),
            keys,
            preferred_element_type=jnp.float32,
        )
        for t in range(across):
            lanes = slice(t * LANES, (t + 1) * LANES)
            acc[:, lanes] = acc[:, lanes] * factor + added[:, lanes]

    for b in range(toks // BLK):
        block, first, clean = scal[b], scal[2 + b], scal[4 + b]
        acc[...] = jnp.zeros_like(acc)
        top[...] = jnp.full_like(top, floor_max)
        mass[...] = jnp.zeros_like(mass)
        count = block - first + 1
        wide = (count + CHUNK - 1) // (2 * CHUNK)

        @pl.loop(0, wide)
        def _(i):
            base = first + i * 2 * CHUNK
            whole = (base >= clean) & (base + 2 * CHUNK <= block)

            @pl.when(whole)
            def _():
                attend(b, base, 2 * CHUNK, False)

            @pl.when(jnp.logical_not(whole))
            def _():
                attend(b, base, 2 * CHUNK, True)

        @pl.when(wide * 2 * CHUNK < count)
        def _():
            attend(b, first + wide * 2 * CHUNK, CHUNK, True)

        total = jnp.sum(mass[...], axis=1, keepdims=True)
        latent_out = (acc[...] / total).astype(jnp.bfloat16)
        done[:, b * BLK : (b + 1) * BLK, :] = latent_out.reshape(heads, BLK, width)

    vh = vup_ref.shape[2]
    for h in range(heads):
        values = jnp.dot(done[h], vup_ref[h], preferred_element_type=jnp.float32).astype(jnp.bfloat16)
        for copy in range(out_ref.shape[0]):
            for at in range(0, toks, OWN):
                to = (at // OWN % 2) * (toks // 2) + at // OWN // 2 * OWN
                out_ref[copy, to : to + OWN, h * vh : (h + 1) * vh] = values[at : at + OWN, :]


def attention(scal, lo, q, vup, lat, copies):
    heads, toks, width = q.shape
    vh = vup.shape[2]
    vmem = pl.BlockSpec(memory_space=pltpu.VMEM)
    return pl.pallas_call(
        attention_kernel,
        out_shape=jax.ShapeDtypeStruct((copies, toks, heads * vh), jnp.bfloat16),
        in_specs=[pl.BlockSpec(memory_space=pltpu.SMEM)] + [vmem] * 4,
        out_specs=vmem,
        scratch_shapes=[
            pltpu.VMEM((2 * CHUNK * BLK, width), jnp.bfloat16),
            pltpu.VMEM((heads * BLK, width), jnp.float32),
            pltpu.VMEM((heads * BLK, LANES), jnp.float32),
            pltpu.VMEM((heads * BLK, LANES), jnp.float32),
            pltpu.VMEM((heads, toks, width), jnp.bfloat16),
        ],
        compiler_params=pltpu.CompilerParams(vmem_limit_bytes=40 * 2**20),
        cost_estimate=pl.CostEstimate(
            flops=6 * 2**30, bytes_accessed=2 * lat.size, transcendentals=2**21
        ),
        name="latent_attention",
    )(scal, lo, q, vup, lat)


def prepare(query, segment_ids, block_of_slot, value_up, seq_index):
    toks, heads, _ = query.shape
    my_blocks = lax.dynamic_slice_in_dim(block_of_slot, 2 * seq_index, 2, 0)
    segs = jnp.concatenate(
        [lax.dynamic_slice_in_dim(segment_ids, my_blocks[i] * BLK, BLK, 0) for i in range(2)]
    )
    lo = jnp.sum((segment_ids[None, :] < segs[:, None]).astype(jnp.int32), axis=1)
    first = lo.reshape(2, BLK)[:, 0] // BLK
    clean = (lo.reshape(2, BLK)[:, BLK - 1] + BLK - 1) // BLK
    first = jnp.concatenate([first, clean])
    n = block_of_slot.shape[0]
    slots = jnp.arange(n, dtype=jnp.int32)
    slot_of_block = jnp.sum(
        jnp.where(block_of_slot[None, :] == slots[:, None], slots[None, :], 0), axis=1
    )
    lo_rows = jnp.broadcast_to(lo[None, :, None], (heads, toks, 1))
    q = query.transpose(1, 0, 2)
    vup = jnp.pad(value_up, ((0, 0), (0, query.shape[2] - value_up.shape[1]), (0, 0)))
    return my_blocks, first, slot_of_block, lo_rows, q, vup


def need_tables(segment_ids, block_of_slot, plane, nzh, halves):
    n = block_of_slot.shape[0]
    firsts = segment_ids.reshape(n, BLK)[:, 0]
    block_first = jnp.sum((segment_ids[None, :] < firsts[:, None]).astype(jnp.int32), axis=1) // BLK
    blocks = jnp.arange(n, dtype=jnp.int32)
    slot_first = jnp.sum(
        jnp.where(block_of_slot[:, None] == blocks[None, :], block_first[None, :], 0), axis=1
    )
    pair = (slot_first[:, None] <= block_of_slot[None, :]) & (
        block_of_slot[None, :] <= block_of_slot[:, None]
    )
    need = jnp.any(pair.reshape(plane, nzh * halves, n), axis=1)
    slot_plane = blocks // halves % nzh
    before = (blocks[:, None] < blocks[None, :]) & (slot_plane[:, None] == slot_plane[None, :])
    rank = jnp.dot(need.astype(jnp.bfloat16), before.astype(jnp.bfloat16), preferred_element_type=jnp.float32)
    most = jnp.max(jnp.where(need, rank, -1.0)) + 1.0
    return need, rank, most <= FEW


def per_device(query, latent, segment_ids, block_of_slot, value_up, out_proj):
    nx, ny, nzh = (lax.axis_size(a) for a in ("x", "y", "zh"))
    nzl, nc = lax.axis_size("zl"), lax.axis_size("core")
    plane = nx * ny
    x, y, zh = (lax.axis_index(a) for a in ("x", "y", "zh"))
    zl, core = lax.axis_index("zl"), lax.axis_index("core")
    seq_index = (x * ny + y) * nzh + zh
    toks, width = latent.shape
    halves, across = toks // BLK, width // LANES
    slices = plane * halves

    cols = out_proj.T
    other = lax.ppermute(cols, "zh", [(i, nzh - 1 - i) for i in range(nzh)])

    number = zl * nc + core
    corner = (0, number // across * ROWS, number % across * LANES)
    part = lax.dynamic_slice(latent.reshape(halves, BLK, width), corner, (halves, ROWS, LANES))
    spread = jnp.broadcast_to(part[None], (plane,) + part.shape)
    plane_rows = lax.all_to_all(spread, ("x", "y"), 0, 0, tiled=True)
    plane_rows = plane_rows.reshape(slices, ROWS * LANES)

    need, rank, fits = need_tables(segment_ids, block_of_slot, plane, nzh, halves)
    my_need = lax.dynamic_index_in_dim(need, x * ny + y, 0, keepdims=False)
    my_rank = lax.dynamic_index_in_dim(rank, x * ny + y, 0, keepdims=False).astype(jnp.int32)
    row_need = lax.dynamic_index_in_dim(my_need.reshape(plane, nzh, halves), zh, 1, keepdims=False)
    row_rank = lax.dynamic_index_in_dim(my_rank.reshape(plane, nzh, halves), zh, 1, keepdims=False)
    row_rank = jnp.where(row_need, row_rank, -1).reshape(1, slices)
    pick = (row_rank == jnp.arange(FEW, dtype=jnp.int32)[:, None]).astype(jnp.bfloat16)
    pick, my_rank = lax.optimization_barrier((pick, my_rank))

    def over_y(piece):
        return lax.all_to_all(jnp.broadcast_to(piece[None], (ny,) + piece.shape), "y", 0, 0, tiled=True)

    def attend(few, operands):
        plane_rows, cols, other, query, segment_ids, block_of_slot, value_up, my_rank, pick = operands
        if few:
            kept = FEW
            sent = jnp.dot(pick, plane_rows, preferred_element_type=jnp.float32).astype(jnp.bfloat16)
        else:
            kept = slices
            sent = plane_rows
        gathered = lax.all_gather(sent.reshape(kept * ROWS, LANES), ("zh", "zl", "core"), axis=0, tiled=True)
        gathered = gathered.reshape(-1, ROWS, LANES)

        cols, other, sent = lax.optimization_barrier((cols, other, sent))
        mine = over_y(cols)
        theirs = over_y(other)

        my_blocks, first, slot_of_block, lo_rows, q, vup = prepare(
            query, segment_ids, block_of_slot, value_up, seq_index
        )
        slot_seq, slot_half = slot_of_block // halves, slot_of_block % halves
        if few:
            slots = jnp.arange(block_of_slot.shape[0], dtype=jnp.int32)
            place = jnp.sum(jnp.where(slot_of_block[:, None] == slots[None, :], my_rank[None, :], 0), axis=1)
            place = jnp.minimum(place, kept - 1)
        else:
            place = slot_seq // nzh * halves + slot_half
        start = (slot_seq % nzh) * PARTS * kept + place
        scal = jnp.concatenate([my_blocks, first, start]).astype(jnp.int32)
        return attention(scal, lo_rows, q, vup, gathered, nx), mine, theirs

    head_values, mine, theirs = lax.cond(
        fits,
        functools.partial(attend, True),
        functools.partial(attend, False),
        (plane_rows, cols, other, query, segment_ids, block_of_slot, value_up, my_rank, pick),
    )

    wide = head_values.shape[2]
    rows = lax.all_to_all(head_values, "x", 0, 0, tiled=True).reshape(nx, nc, toks // nc, wide)
    columns = jnp.where(zh == 0, jnp.stack([mine, theirs], 1), jnp.stack([theirs, mine], 1))
    columns = columns.reshape(-1, cols.shape[1])
    n_cols = columns.shape[0]
    own = toks // (nzl * nc)

    def project(which):
        part = lax.dynamic_index_in_dim(rows, which, 1, keepdims=False)
        return lax.dot_general(
            part.reshape(-1, wide), columns, (((1,), (1,)), ((), ())), preferred_element_type=jnp.float32
        )

    give = project(nc - 1 - core).astype(jnp.bfloat16)
    got = lax.ppermute(give, "core", [(i, nc - 1 - i) for i in range(nc)])
    chip = (project(core) + got.astype(jnp.float32)).astype(jnp.bfloat16)
    chip = chip.reshape(nx * nzl, own, n_cols)
    terms = lax.all_to_all(chip, ("x", "zl"), 0, 0, tiled=True)
    terms = terms.reshape(nx, nzl, own, n_cols).astype(jnp.float32)
    mixed = jnp.sum(terms, axis=1).astype(jnp.bfloat16)
    return mixed.transpose(1, 0, 2).reshape(own, nx * n_cols)


AXES = {"x": 4, "y": 8, "zh": 2, "zl": 4, "core": 2}


def solution(mesh):
    names = tuple(AXES)
    fine = Mesh(mesh.devices.reshape(tuple(AXES.values())), names)
    seq, head = names[:3], names[3:]
    return jax.shard_map(
        per_device,
        mesh=fine,
        in_specs=(
            P(seq, head, None),
            P(seq, None),
            P(),
            P(),
            P(head, None, None),
            P(head, seq),
        ),
        out_specs=P(names, None),
        check_vma=False,
    )
```

```python
import functools
import math

import jax
import jax.numpy as jnp
from jax import lax
from jax.experimental import pallas as pl
from jax.experimental.pallas import tpu as pltpu
from jax.sharding import Mesh
from jax.sharding import PartitionSpec as P

BLK = 64
CHUNK = 8
ROWS, LANES = 32, 128
PARTS = 8
OWN = 16
LEVELS = (40, 48)
exp2_scale = 192 ** (-0.5) * math.log2(math.e)
floor_max = -1e30
masked_score = -2e30


def attention_kernel(scal, lo_ref, q_ref, vup_ref, lat, out_ref, kbuf, acc, top, mass, done):
    heads, toks, width = q_ref.shape
    rows = heads * BLK
    slices = lat.shape[0] // 16
    across = width // LANES
    n_blocks = scal.shape[0] - 6

    def attend(b, base, size, masked):
        for j in range(size):
            src = scal[6 + jnp.minimum(base + j, n_blocks - 1)]
            for part in range(PARTS):
                row = j * BLK + part // across * ROWS
                lane = part % across * LANES
                kbuf[row : row + ROWS, lane : lane + LANES] = lat[src + part * slices]
        keys = kbuf[: size * BLK, :]
        q = q_ref[:, b * BLK : (b + 1) * BLK, :].reshape(rows, width)
        s = lax.dot_general(q, keys, (((1,), (1,)), ((), ())), preferred_element_type=jnp.float32)
        if masked:
            lo = lo_ref[:, b * BLK : (b + 1) * BLK, :].reshape(rows, 1)
            pos = scal[b] * BLK + lax.broadcasted_iota(jnp.int32, (heads, BLK, 1), 1).reshape(rows, 1)
            kp = base * BLK + lax.broadcasted_iota(jnp.int32, (1, size * BLK), 1)
            s = jnp.where((kp <= pos) & (kp >= lo), s, masked_score)
        tiles = [s[:, t : t + LANES] for t in range(0, size * BLK, LANES)]
        old = top[...]
        new = jnp.maximum(old, jnp.max(functools.reduce(jnp.maximum, tiles), axis=1, keepdims=True))
        factor = jnp.exp2((old - new) * exp2_scale)
        w = [jnp.exp2((tile - new) * exp2_scale) for tile in tiles]
        top[...] = new
        mass[...] = mass[...] * factor + functools.reduce(jnp.add, w)
        added = jnp.dot(
            jnp.concatenate([x.astype(jnp.bfloat16) for x in w], axis=1),
            keys,
            preferred_element_type=jnp.float32,
        )
        for t in range(across):
            lanes = slice(t * LANES, (t + 1) * LANES)
            acc[:, lanes] = acc[:, lanes] * factor + added[:, lanes]

    for b in range(toks // BLK):
        block, first, clean = scal[b], scal[2 + b], scal[4 + b]
        acc[...] = jnp.zeros_like(acc)
        top[...] = jnp.full_like(top, floor_max)
        mass[...] = jnp.zeros_like(mass)
        count = block - first + 1
        wide = (count + CHUNK - 1) // (2 * CHUNK)

        @pl.loop(0, wide)
        def _(i):
            base = first + i * 2 * CHUNK
            whole = (base >= clean) & (base + 2 * CHUNK <= block)

            @pl.when(whole)
            def _():
                attend(b, base, 2 * CHUNK, False)

            @pl.when(jnp.logical_not(whole))
            def _():
                attend(b, base, 2 * CHUNK, True)

        @pl.when(wide * 2 * CHUNK < count)
        def _():
            attend(b, first + wide * 2 * CHUNK, CHUNK, True)

        total = jnp.sum(mass[...], axis=1, keepdims=True)
        latent_out = (acc[...] / total).astype(jnp.bfloat16)
        done[:, b * BLK : (b + 1) * BLK, :] = latent_out.reshape(heads, BLK, width)

    vh = vup_ref.shape[2]
    for h in range(heads):
        values = jnp.dot(done[h], vup_ref[h], preferred_element_type=jnp.float32).astype(jnp.bfloat16)
        for copy in range(out_ref.shape[0]):
            for at in range(0, toks, OWN):
                to = (at // OWN % 2) * (toks // 2) + at // OWN // 2 * OWN
                out_ref[copy, to : to + OWN, h * vh : (h + 1) * vh] = values[at : at + OWN, :]


def attention(scal, lo, q, vup, lat, copies):
    heads, toks, width = q.shape
    vh = vup.shape[2]
    vmem = pl.BlockSpec(memory_space=pltpu.VMEM)
    return pl.pallas_call(
        attention_kernel,
        out_shape=jax.ShapeDtypeStruct((copies, toks, heads * vh), jnp.bfloat16),
        in_specs=[pl.BlockSpec(memory_space=pltpu.SMEM)] + [vmem] * 4,
        out_specs=vmem,
        scratch_shapes=[
            pltpu.VMEM((2 * CHUNK * BLK, width), jnp.bfloat16),
            pltpu.VMEM((heads * BLK, width), jnp.float32),
            pltpu.VMEM((heads * BLK, LANES), jnp.float32),
            pltpu.VMEM((heads * BLK, LANES), jnp.float32),
            pltpu.VMEM((heads, toks, width), jnp.bfloat16),
        ],
        compiler_params=pltpu.CompilerParams(vmem_limit_bytes=40 * 2**20),
        cost_estimate=pl.CostEstimate(
            flops=6 * 2**30, bytes_accessed=2 * lat.size, transcendentals=2**21
        ),
        name="latent_attention",
    )(scal, lo, q, vup, lat)


def prepare(query, segment_ids, block_of_slot, value_up, seq_index):
    toks, heads, _ = query.shape
    my_blocks = lax.dynamic_slice_in_dim(block_of_slot, 2 * seq_index, 2, 0)
    segs = jnp.concatenate(
        [lax.dynamic_slice_in_dim(segment_ids, my_blocks[i] * BLK, BLK, 0) for i in range(2)]
    )
    lo = jnp.sum((segment_ids[None, :] < segs[:, None]).astype(jnp.int32), axis=1)
    first = lo.reshape(2, BLK)[:, 0] // BLK
    clean = (lo.reshape(2, BLK)[:, BLK - 1] + BLK - 1) // BLK
    first = jnp.concatenate([first, clean])
    n = block_of_slot.shape[0]
    slots = jnp.arange(n, dtype=jnp.int32)
    slot_of_block = jnp.sum(
        jnp.where(block_of_slot[None, :] == slots[:, None], slots[None, :], 0), axis=1
    )
    lo_rows = jnp.broadcast_to(lo[None, :, None], (heads, toks, 1))
    q = query.transpose(1, 0, 2)
    vup = jnp.pad(value_up, ((0, 0), (0, query.shape[2] - value_up.shape[1]), (0, 0)))
    return my_blocks, first, slot_of_block, lo_rows, q, vup


def need_tables(segment_ids, block_of_slot, plane, nzh, halves):
    n = block_of_slot.shape[0]
    firsts = segment_ids.reshape(n, BLK)[:, 0]
    block_first = jnp.sum((segment_ids[None, :] < firsts[:, None]).astype(jnp.int32), axis=1) // BLK
    blocks = jnp.arange(n, dtype=jnp.int32)
    slot_first = jnp.sum(
        jnp.where(block_of_slot[:, None] == blocks[None, :], block_first[None, :], 0), axis=1
    )
    pair = (slot_first[:, None] <= block_of_slot[None, :]) & (
        block_of_slot[None, :] <= block_of_slot[:, None]
    )
    need = jnp.any(pair.reshape(plane, nzh * halves, n), axis=1)
    slot_plane = blocks // halves % nzh
    before = (blocks[:, None] < blocks[None, :]) & (slot_plane[:, None] == slot_plane[None, :])
    rank = jnp.dot(need.astype(jnp.bfloat16), before.astype(jnp.bfloat16), preferred_element_type=jnp.float32)
    most = jnp.max(jnp.where(need, rank, -1.0)) + 1.0
    level = sum((most > kept).astype(jnp.int32) for kept in LEVELS)
    return need, rank, level


def per_device(query, latent, segment_ids, block_of_slot, value_up, out_proj):
    nx, ny, nzh = (lax.axis_size(a) for a in ("x", "y", "zh"))
    nzl, nc = lax.axis_size("zl"), lax.axis_size("core")
    plane = nx * ny
    x, y, zh = (lax.axis_index(a) for a in ("x", "y", "zh"))
    zl, core = lax.axis_index("zl"), lax.axis_index("core")
    seq_index = (x * ny + y) * nzh + zh
    toks, width = latent.shape
    halves, across = toks // BLK, width // LANES
    slices = plane * halves

    cols = out_proj.T
    other = lax.ppermute(cols, "zh", [(i, nzh - 1 - i) for i in range(nzh)])

    number = zl * nc + core
    corner = (0, number // across * ROWS, number % across * LANES)
    part = lax.dynamic_slice(latent.reshape(halves, BLK, width), corner, (halves, ROWS, LANES))
    spread = jnp.broadcast_to(part[None], (plane,) + part.shape)
    plane_rows = lax.all_to_all(spread, ("x", "y"), 0, 0, tiled=True)
    plane_rows = plane_rows.reshape(slices, ROWS * LANES)

    need, rank, level = need_tables(segment_ids, block_of_slot, plane, nzh, halves)
    my_need = lax.dynamic_index_in_dim(need, x * ny + y, 0, keepdims=False)
    my_rank = lax.dynamic_index_in_dim(rank, x * ny + y, 0, keepdims=False).astype(jnp.int32)
    row_need = lax.dynamic_index_in_dim(my_need.reshape(plane, nzh, halves), zh, 1, keepdims=False)
    row_rank = lax.dynamic_index_in_dim(my_rank.reshape(plane, nzh, halves), zh, 1, keepdims=False)
    row_rank = jnp.where(row_need, row_rank, -1).reshape(1, slices)
    pick = (row_rank == jnp.arange(LEVELS[-1], dtype=jnp.int32)[:, None]).astype(jnp.bfloat16)
    pick, my_rank = lax.optimization_barrier((pick, my_rank))

    def over_y(piece):
        return lax.all_to_all(jnp.broadcast_to(piece[None], (ny,) + piece.shape), "y", 0, 0, tiled=True)

    def attend(kept, operands):
        plane_rows, cols, other, query, segment_ids, block_of_slot, value_up, my_rank, pick = operands
        few = kept < slices
        sent = plane_rows
        if few:
            sent = jnp.dot(pick[:kept], plane_rows, preferred_element_type=jnp.float32).astype(jnp.bfloat16)
        gathered = lax.all_gather(sent.reshape(kept * ROWS, LANES), ("zh", "zl", "core"), axis=0, tiled=True)
        gathered = gathered.reshape(-1, ROWS, LANES)

        cols, other, sent = lax.optimization_barrier((cols, other, sent))
        mine = over_y(cols)
        theirs = over_y(other)

        my_blocks, first, slot_of_block, lo_rows, q, vup = prepare(
            query, segment_ids, block_of_slot, value_up, seq_index
        )
        slot_seq, slot_half = slot_of_block // halves, slot_of_block % halves
        if few:
            slots = jnp.arange(block_of_slot.shape[0], dtype=jnp.int32)
            place = jnp.sum(jnp.where(slot_of_block[:, None] == slots[None, :], my_rank[None, :], 0), axis=1)
            place = jnp.minimum(place, kept - 1)
        else:
            place = slot_seq // nzh * halves + slot_half
        start = (slot_seq % nzh) * PARTS * kept + place
        scal = jnp.concatenate([my_blocks, first, start]).astype(jnp.int32)
        return attention(scal, lo_rows, q, vup, gathered, nx), mine, theirs

    head_values, mine, theirs = lax.switch(
        level,
        [functools.partial(attend, kept) for kept in (*LEVELS, slices)],
        (plane_rows, cols, other, query, segment_ids, block_of_slot, value_up, my_rank, pick),
    )

    wide = head_values.shape[2]
    rows = lax.all_to_all(head_values, "x", 0, 0, tiled=True).reshape(nx, nc, toks // nc, wide)
    columns = jnp.where(zh == 0, jnp.stack([mine, theirs], 1), jnp.stack([theirs, mine], 1))
    columns = columns.reshape(-1, cols.shape[1])
    n_cols = columns.shape[0]
    own = toks // (nzl * nc)

    def project(which):
        part = lax.dynamic_index_in_dim(rows, which, 1, keepdims=False)
        return lax.dot_general(
            part.reshape(-1, wide), columns, (((1,), (1,)), ((), ())), preferred_element_type=jnp.float32
        )

    give = project(nc - 1 - core).astype(jnp.bfloat16)
    got = lax.ppermute(give, "core", [(i, nc - 1 - i) for i in range(nc)])
    keep = lax.optimization_barrier(project(core))
    chip = (keep + got.astype(jnp.float32)).astype(jnp.bfloat16)
    chip = chip.reshape(nx * nzl, own, n_cols)
    terms = lax.all_to_all(chip, ("x", "zl"), 0, 0, tiled=True)
    terms = terms.reshape(nx, nzl, own, n_cols)
    sums = [functools.reduce(jnp.add, [terms[i, j].astype(jnp.float32) for j in range(nzl)]) for i in range(nx)]
    return jnp.concatenate([each.astype(jnp.bfloat16) for each in sums], axis=1)


AXES = {"x": 4, "y": 8, "zh": 2, "zl": 4, "core": 2}


def solution(mesh):
    names = tuple(AXES)
    fine = Mesh(mesh.devices.reshape(tuple(AXES.values())), names)
    seq, head = names[:3], names[3:]
    return jax.shard_map(
        per_device,
        mesh=fine,
        in_specs=(
            P(seq, head, None),
            P(seq, None),
            P(),
            P(),
            P(head, None, None),
            P(head, seq),
        ),
        out_specs=P(names, None),
        check_vma=False,
    )
```

```python
import functools
import math

import jax
import jax.numpy as jnp
from jax import lax
from jax.experimental import pallas as pl
from jax.experimental.pallas import tpu as pltpu
from jax.sharding import Mesh
from jax.sharding import PartitionSpec as P

BLK = 64
CHUNK = 8
ROWS, LANES = 32, 128
PARTS = 8
OWN = 16
LEVELS = (40, 48)
exp2_scale = 192 ** (-0.5) * math.log2(math.e)
floor_max = -1e30
masked_score = -2e30


def attention_kernel(scal, lo_ref, q_ref, vup_ref, lat, out_ref, kbuf, acc, top, mass, done):
    heads, toks, width = q_ref.shape
    rows = heads * BLK
    slices = lat.shape[0] // 16
    across = width // LANES
    n_blocks = scal.shape[0] - 6

    def attend(b, base, size, masked):
        for j in range(size):
            src = scal[6 + jnp.minimum(base + j, n_blocks - 1)]
            for part in range(PARTS):
                row = j * BLK + part // across * ROWS
                lane = part % across * LANES
                kbuf[row : row + ROWS, lane : lane + LANES] = lat[src + part * slices]
        keys = kbuf[: size * BLK, :]
        q = q_ref[:, b * BLK : (b + 1) * BLK, :].reshape(rows, width)
        s = lax.dot_general(q, keys, (((1,), (1,)), ((), ())), preferred_element_type=jnp.float32)
        if masked:
            lo = lo_ref[:, b * BLK : (b + 1) * BLK, :].reshape(rows, 1)
            pos = scal[b] * BLK + lax.broadcasted_iota(jnp.int32, (heads, BLK, 1), 1).reshape(rows, 1)
            kp = base * BLK + lax.broadcasted_iota(jnp.int32, (1, size * BLK), 1)
            s = jnp.where((kp <= pos) & (kp >= lo), s, masked_score)
        tiles = [s[:, t : t + LANES] for t in range(0, size * BLK, LANES)]
        old = top[...]
        new = jnp.maximum(old, jnp.max(functools.reduce(jnp.maximum, tiles), axis=1, keepdims=True))
        factor = jnp.exp2((old - new) * exp2_scale)
        w = [jnp.exp2((tile - new) * exp2_scale) for tile in tiles]
        top[...] = new
        mass[...] = mass[...] * factor + functools.reduce(jnp.add, w)
        added = jnp.dot(
            jnp.concatenate([x.astype(jnp.bfloat16) for x in w], axis=1),
            keys,
            preferred_element_type=jnp.float32,
        )
        for t in range(across):
            lanes = slice(t * LANES, (t + 1) * LANES)
            acc[:, lanes] = acc[:, lanes] * factor + added[:, lanes]

    for b in range(toks // BLK):
        block, first, clean = scal[b], scal[2 + b], scal[4 + b]
        acc[...] = jnp.zeros_like(acc)
        top[...] = jnp.full_like(top, floor_max)
        mass[...] = jnp.zeros_like(mass)
        count = block - first + 1
        wide = (count + CHUNK - 1) // (2 * CHUNK)

        @pl.loop(0, wide)
        def _(i):
            base = first + i * 2 * CHUNK
            whole = (base >= clean) & (base + 2 * CHUNK <= block)

            @pl.when(whole)
            def _():
                attend(b, base, 2 * CHUNK, False)

            @pl.when(jnp.logical_not(whole))
            def _():
                attend(b, base, 2 * CHUNK, True)

        @pl.when(wide * 2 * CHUNK < count)
        def _():
            attend(b, first + wide * 2 * CHUNK, CHUNK, True)

        total = jnp.sum(mass[...], axis=1, keepdims=True)
        latent_out = (acc[...] / total).astype(jnp.bfloat16)
        done[:, b * BLK : (b + 1) * BLK, :] = latent_out.reshape(heads, BLK, width)

    vh = vup_ref.shape[2]
    for h in range(heads):
        values = jnp.dot(done[h], vup_ref[h], preferred_element_type=jnp.float32).astype(jnp.bfloat16)
        for copy in range(out_ref.shape[0]):
            for at in range(0, toks, OWN):
                to = (at // OWN % 2) * (toks // 2) + at // OWN // 2 * OWN
                out_ref[copy, to : to + OWN, h * vh : (h + 1) * vh] = values[at : at + OWN, :]


def attention(scal, lo, q, vup, lat, copies):
    heads, toks, width = q.shape
    vh = vup.shape[2]
    vmem = pl.BlockSpec(memory_space=pltpu.VMEM)
    return pl.pallas_call(
        attention_kernel,
        out_shape=jax.ShapeDtypeStruct((copies, toks, heads * vh), jnp.bfloat16),
        in_specs=[pl.BlockSpec(memory_space=pltpu.SMEM)] + [vmem] * 4,
        out_specs=vmem,
        scratch_shapes=[
            pltpu.VMEM((2 * CHUNK * BLK, width), jnp.bfloat16),
            pltpu.VMEM((heads * BLK, width), jnp.float32),
            pltpu.VMEM((heads * BLK, LANES), jnp.float32),
            pltpu.VMEM((heads * BLK, LANES), jnp.float32),
            pltpu.VMEM((heads, toks, width), jnp.bfloat16),
        ],
        compiler_params=pltpu.CompilerParams(vmem_limit_bytes=40 * 2**20),
        cost_estimate=pl.CostEstimate(
            flops=6 * 2**30, bytes_accessed=2 * lat.size, transcendentals=2**21
        ),
        name="latent_attention",
    )(scal, lo, q, vup, lat)


def prepare(query, segment_ids, block_of_slot, value_up, seq_index):
    toks, heads, _ = query.shape
    my_blocks = lax.dynamic_slice_in_dim(block_of_slot, 2 * seq_index, 2, 0)
    segs = jnp.concatenate(
        [lax.dynamic_slice_in_dim(segment_ids, my_blocks[i] * BLK, BLK, 0) for i in range(2)]
    )
    lo = jnp.sum((segment_ids[None, :] < segs[:, None]).astype(jnp.int32), axis=1)
    first = lo.reshape(2, BLK)[:, 0] // BLK
    clean = (lo.reshape(2, BLK)[:, BLK - 1] + BLK - 1) // BLK
    first = jnp.concatenate([first, clean])
    n = block_of_slot.shape[0]
    slots = jnp.arange(n, dtype=jnp.int32)
    slot_of_block = jnp.sum(
        jnp.where(block_of_slot[None, :] == slots[:, None], slots[None, :], 0), axis=1
    )
    lo_rows = jnp.broadcast_to(lo[None, :, None], (heads, toks, 1))
    q = query.transpose(1, 0, 2)
    vup = jnp.pad(value_up, ((0, 0), (0, query.shape[2] - value_up.shape[1]), (0, 0)))
    return my_blocks, first, slot_of_block, lo_rows, q, vup


def need_tables(segment_ids, block_of_slot, plane, nzh, halves):
    n = block_of_slot.shape[0]
    firsts = segment_ids.reshape(n, BLK)[:, 0]
    block_first = jnp.sum((segment_ids[None, :] < firsts[:, None]).astype(jnp.int32), axis=1) // BLK
    blocks = jnp.arange(n, dtype=jnp.int32)
    slot_first = jnp.sum(
        jnp.where(block_of_slot[:, None] == blocks[None, :], block_first[None, :], 0), axis=1
    )
    pair = (slot_first[:, None] <= block_of_slot[None, :]) & (
        block_of_slot[None, :] <= block_of_slot[:, None]
    )
    need = jnp.any(pair.reshape(plane, nzh * halves, n), axis=1)
    slot_plane = blocks // halves % nzh
    before = (blocks[:, None] < blocks[None, :]) & (slot_plane[:, None] == slot_plane[None, :])
    rank = jnp.dot(need.astype(jnp.bfloat16), before.astype(jnp.bfloat16), preferred_element_type=jnp.float32)
    most = jnp.max(jnp.where(need, rank, -1.0)) + 1.0
    level = sum((most > kept).astype(jnp.int32) for kept in LEVELS)
    return need, rank, level


def per_device(query, latent, segment_ids, block_of_slot, value_up, out_proj):
    nx, ny, nzh = (lax.axis_size(a) for a in ("x", "y", "zh"))
    nzl, nc = lax.axis_size("zl"), lax.axis_size("core")
    plane = nx * ny
    x, y, zh = (lax.axis_index(a) for a in ("x", "y", "zh"))
    zl, core = lax.axis_index("zl"), lax.axis_index("core")
    seq_index = (x * ny + y) * nzh + zh
    toks, width = latent.shape
    halves, across = toks // BLK, width // LANES
    slices = plane * halves

    cols = out_proj.T
    other = lax.ppermute(cols, "zh", [(i, nzh - 1 - i) for i in range(nzh)])

    number = zl * nc + core
    corner = (0, number // across * ROWS, number % across * LANES)
    part = lax.dynamic_slice(latent.reshape(halves, BLK, width), corner, (halves, ROWS, LANES))
    spread = jnp.broadcast_to(part[None], (plane,) + part.shape)
    plane_rows = lax.all_to_all(spread, ("x", "y"), 0, 0, tiled=True)
    plane_rows = plane_rows.reshape(slices, ROWS * LANES)

    need, rank, level = need_tables(segment_ids, block_of_slot, plane, nzh, halves)
    my_need = lax.dynamic_index_in_dim(need, x * ny + y, 0, keepdims=False)
    my_rank = lax.dynamic_index_in_dim(rank, x * ny + y, 0, keepdims=False).astype(jnp.int32)
    row_need = lax.dynamic_index_in_dim(my_need.reshape(plane, nzh, halves), zh, 1, keepdims=False)
    row_rank = lax.dynamic_index_in_dim(my_rank.reshape(plane, nzh, halves), zh, 1, keepdims=False)
    row_rank = jnp.where(row_need, row_rank, -1).reshape(1, slices)
    pick = (row_rank == jnp.arange(LEVELS[-1], dtype=jnp.int32)[:, None]).astype(jnp.bfloat16)
    pick, my_rank = lax.optimization_barrier((pick, my_rank))

    def over_y(piece):
        return lax.all_gather(piece, "y", axis=0)

    def attend(kept, operands):
        plane_rows, cols, other, query, segment_ids, block_of_slot, value_up, my_rank, pick = operands
        few = kept < slices
        sent = plane_rows
        if few:
            sent = jnp.dot(pick[:kept], plane_rows, preferred_element_type=jnp.float32).astype(jnp.bfloat16)
        gathered = lax.all_gather(sent.reshape(kept * ROWS, LANES), ("zh", "zl", "core"), axis=0, tiled=True)
        gathered = gathered.reshape(-1, ROWS, LANES)

        cols, other, sent = lax.optimization_barrier((cols, other, sent))
        mine = over_y(cols)
        theirs = over_y(other)

        my_blocks, first, slot_of_block, lo_rows, q, vup = prepare(
            query, segment_ids, block_of_slot, value_up, seq_index
        )
        slot_seq, slot_half = slot_of_block // halves, slot_of_block % halves
        if few:
            slots = jnp.arange(block_of_slot.shape[0], dtype=jnp.int32)
            place = jnp.sum(jnp.where(slot_of_block[:, None] == slots[None, :], my_rank[None, :], 0), axis=1)
            place = jnp.minimum(place, kept - 1)
        else:
            place = slot_seq // nzh * halves + slot_half
        start = (slot_seq % nzh) * PARTS * kept + place
        scal = jnp.concatenate([my_blocks, first, start]).astype(jnp.int32)
        return attention(scal, lo_rows, q, vup, gathered, nx), mine, theirs

    head_values, mine, theirs = lax.switch(
        level,
        [functools.partial(attend, kept) for kept in (*LEVELS, slices)],
        (plane_rows, cols, other, query, segment_ids, block_of_slot, value_up, my_rank, pick),
    )

    wide = head_values.shape[2]
    rows = lax.all_to_all(head_values, "x", 0, 0, tiled=True).reshape(nx, nc, toks // nc, wide)
    columns = jnp.where(zh == 0, jnp.stack([mine, theirs], 1), jnp.stack([theirs, mine], 1))
    columns = columns.reshape(-1, cols.shape[1])
    n_cols = columns.shape[0]
    own = toks // (nzl * nc)

    def project(which):
        part = lax.dynamic_index_in_dim(rows, which, 1, keepdims=False)
        return lax.dot_general(
            part.reshape(-1, wide), columns, (((1,), (1,)), ((), ())), preferred_element_type=jnp.float32
        )

    give = project(nc - 1 - core).astype(jnp.bfloat16)
    got = lax.ppermute(give, "core", [(i, nc - 1 - i) for i in range(nc)])
    keep = lax.optimization_barrier(project(core))
    chip = (keep + got.astype(jnp.float32)).astype(jnp.bfloat16)
    chip = chip.reshape(nx * nzl, own, n_cols)
    terms = lax.all_to_all(chip, ("x", "zl"), 0, 0, tiled=True)
    terms = terms.reshape(nx, nzl, own, n_cols)
    sums = [functools.reduce(jnp.add, [terms[i, j].astype(jnp.float32) for j in range(nzl)]) for i in range(nx)]
    return jnp.concatenate([each.astype(jnp.bfloat16) for each in sums], axis=1)


AXES = {"x": 4, "y": 8, "zh": 2, "zl": 4, "core": 2}


def solution(mesh):
    names = tuple(AXES)
    fine = Mesh(mesh.devices.reshape(tuple(AXES.values())), names)
    seq, head = names[:3], names[3:]
    return jax.shard_map(
        per_device,
        mesh=fine,
        in_specs=(
            P(seq, head, None),
            P(seq, None),
            P(),
            P(),
            P(head, None, None),
            P(head, seq),
        ),
        out_specs=P(names, None),
        check_vma=False,
    )
```

```python
import functools
import math

import jax
import jax.numpy as jnp
from jax import lax
from jax.experimental import pallas as pl
from jax.experimental.pallas import tpu as pltpu
from jax.sharding import Mesh
from jax.sharding import PartitionSpec as P

BLK = 64
CHUNK = 8
ROWS, LANES = 32, 128
PARTS = 8
OWN = 16
LEVELS = (40, 48)
exp2_scale = 192 ** (-0.5) * math.log2(math.e)
floor_max = -1e30
masked_score = -2e30


def attention_kernel(scal, lo_ref, q_ref, vup_ref, lat, out_ref, kbuf, acc, top, mass, done):
    heads, toks, width = q_ref.shape
    rows = heads * BLK
    slices = lat.shape[0] // 16
    across = width // LANES
    n_blocks = scal.shape[0] - 6

    def attend(b, base, size, masked):
        for j in range(size):
            src = scal[6 + jnp.minimum(base + j, n_blocks - 1)]
            for part in range(PARTS):
                row = j * BLK + part // across * ROWS
                lane = part % across * LANES
                kbuf[row : row + ROWS, lane : lane + LANES] = lat[src + part * slices]
        keys = kbuf[: size * BLK, :]
        q = q_ref[:, b * BLK : (b + 1) * BLK, :].reshape(rows, width)
        s = lax.dot_general(q, keys, (((1,), (1,)), ((), ())), preferred_element_type=jnp.float32)
        if masked:
            lo = lo_ref[:, b * BLK : (b + 1) * BLK, :].reshape(rows, 1)
            pos = scal[b] * BLK + lax.broadcasted_iota(jnp.int32, (heads, BLK, 1), 1).reshape(rows, 1)
            kp = base * BLK + lax.broadcasted_iota(jnp.int32, (1, size * BLK), 1)
            s = jnp.where((kp <= pos) & (kp >= lo), s, masked_score)
        tiles = [s[:, t : t + LANES] for t in range(0, size * BLK, LANES)]
        old = top[...]
        new = jnp.maximum(old, jnp.max(functools.reduce(jnp.maximum, tiles), axis=1, keepdims=True))
        factor = jnp.exp2((old - new) * exp2_scale)
        w = [jnp.exp2((tile - new) * exp2_scale) for tile in tiles]
        top[...] = new
        mass[...] = mass[...] * factor + functools.reduce(jnp.add, w)
        added = jnp.dot(
            jnp.concatenate([x.astype(jnp.bfloat16) for x in w], axis=1),
            keys,
            preferred_element_type=jnp.float32,
        )
        for t in range(across):
            lanes = slice(t * LANES, (t + 1) * LANES)
            acc[:, lanes] = acc[:, lanes] * factor + added[:, lanes]

    for b in range(toks // BLK):
        block, first, clean = scal[b], scal[2 + b], scal[4 + b]
        acc[...] = jnp.zeros_like(acc)
        top[...] = jnp.full_like(top, floor_max)
        mass[...] = jnp.zeros_like(mass)
        count = block - first + 1
        wide = (count + CHUNK - 1) // (2 * CHUNK)

        @pl.loop(0, wide)
        def _(i):
            base = first + i * 2 * CHUNK
            whole = (base >= clean) & (base + 2 * CHUNK <= block)

            @pl.when(whole)
            def _():
                attend(b, base, 2 * CHUNK, False)

            @pl.when(jnp.logical_not(whole))
            def _():
                attend(b, base, 2 * CHUNK, True)

        @pl.when(wide * 2 * CHUNK < count)
        def _():
            attend(b, first + wide * 2 * CHUNK, CHUNK, True)

        total = jnp.sum(mass[...], axis=1, keepdims=True)
        latent_out = (acc[...] / total).astype(jnp.bfloat16)
        done[:, b * BLK : (b + 1) * BLK, :] = latent_out.reshape(heads, BLK, width)

    vh = vup_ref.shape[2]
    for h in range(heads):
        values = jnp.dot(done[h], vup_ref[h], preferred_element_type=jnp.float32).astype(jnp.bfloat16)
        for copy in range(out_ref.shape[0]):
            for at in range(0, toks, OWN):
                to = (at // OWN % 2) * (toks // 2) + at // OWN // 2 * OWN
                out_ref[copy, to : to + OWN, h * vh : (h + 1) * vh] = values[at : at + OWN, :]


def attention(scal, lo, q, vup, lat, copies):
    heads, toks, width = q.shape
    vh = vup.shape[2]
    vmem = pl.BlockSpec(memory_space=pltpu.VMEM)
    return pl.pallas_call(
        attention_kernel,
        out_shape=jax.ShapeDtypeStruct((copies, toks, heads * vh), jnp.bfloat16),
        in_specs=[pl.BlockSpec(memory_space=pltpu.SMEM)] + [vmem] * 4,
        out_specs=vmem,
        scratch_shapes=[
            pltpu.VMEM((2 * CHUNK * BLK, width), jnp.bfloat16),
            pltpu.VMEM((heads * BLK, width), jnp.float32),
            pltpu.VMEM((heads * BLK, LANES), jnp.float32),
            pltpu.VMEM((heads * BLK, LANES), jnp.float32),
            pltpu.VMEM((heads, toks, width), jnp.bfloat16),
        ],
        compiler_params=pltpu.CompilerParams(vmem_limit_bytes=40 * 2**20),
        cost_estimate=pl.CostEstimate(
            flops=6 * 2**30, bytes_accessed=2 * lat.size, transcendentals=2**21
        ),
        name="latent_attention",
    )(scal, lo, q, vup, lat)


def prepare(query, segment_ids, block_of_slot, value_up, seq_index):
    toks, heads, _ = query.shape
    my_blocks = lax.dynamic_slice_in_dim(block_of_slot, 2 * seq_index, 2, 0)
    segs = jnp.concatenate(
        [lax.dynamic_slice_in_dim(segment_ids, my_blocks[i] * BLK, BLK, 0) for i in range(2)]
    )
    lo = jnp.sum((segment_ids[None, :] < segs[:, None]).astype(jnp.int32), axis=1)
    first = lo.reshape(2, BLK)[:, 0] // BLK
    clean = (lo.reshape(2, BLK)[:, BLK - 1] + BLK - 1) // BLK
    first = jnp.concatenate([first, clean])
    n = block_of_slot.shape[0]
    slots = jnp.arange(n, dtype=jnp.int32)
    slot_of_block = jnp.sum(
        jnp.where(block_of_slot[None, :] == slots[:, None], slots[None, :], 0), axis=1
    )
    lo_rows = jnp.broadcast_to(lo[None, :, None], (heads, toks, 1))
    q = query.transpose(1, 0, 2)
    vup = jnp.pad(value_up, ((0, 0), (0, query.shape[2] - value_up.shape[1]), (0, 0)))
    return my_blocks, first, slot_of_block, lo_rows, q, vup


def need_tables(segment_ids, block_of_slot, plane, nzh, halves):
    n = block_of_slot.shape[0]
    firsts = segment_ids.reshape(n, BLK)[:, 0]
    block_first = jnp.sum((segment_ids[None, :] < firsts[:, None]).astype(jnp.int32), axis=1) // BLK
    blocks = jnp.arange(n, dtype=jnp.int32)
    slot_first = jnp.sum(
        jnp.where(block_of_slot[:, None] == blocks[None, :], block_first[None, :], 0), axis=1
    )
    pair = (slot_first[:, None] <= block_of_slot[None, :]) & (
        block_of_slot[None, :] <= block_of_slot[:, None]
    )
    need = jnp.any(pair.reshape(plane, nzh * halves, n), axis=1)
    slot_plane = blocks // halves % nzh
    before = (blocks[:, None] < blocks[None, :]) & (slot_plane[:, None] == slot_plane[None, :])
    rank = jnp.dot(need.astype(jnp.bfloat16), before.astype(jnp.bfloat16), preferred_element_type=jnp.float32)
    most = jnp.max(jnp.where(need, rank, -1.0)) + 1.0
    level = sum((most > kept).astype(jnp.int32) for kept in LEVELS)
    return need, rank, level


def per_device(query, latent, segment_ids, block_of_slot, value_up, out_proj):
    nx, ny, nzh = (lax.axis_size(a) for a in ("x", "y", "zh"))
    nzl, nc = lax.axis_size("zl"), lax.axis_size("core")
    plane = nx * ny
    x, y, zh = (lax.axis_index(a) for a in ("x", "y", "zh"))
    zl, core = lax.axis_index("zl"), lax.axis_index("core")
    seq_index = (x * ny + y) * nzh + zh
    toks, width = latent.shape
    halves, across = toks // BLK, width // LANES
    slices = plane * halves

    cols = out_proj.T

    number = zl * nc + core
    corner = (0, number // across * ROWS, number % across * LANES)
    part = lax.dynamic_slice(latent.reshape(halves, BLK, width), corner, (halves, ROWS, LANES))
    spread = jnp.broadcast_to(part[None], (plane,) + part.shape)
    plane_rows = lax.all_to_all(spread, ("x", "y"), 0, 0, tiled=True)
    plane_rows = plane_rows.reshape(slices, ROWS * LANES)

    need, rank, level = need_tables(segment_ids, block_of_slot, plane, nzh, halves)
    my_need = lax.dynamic_index_in_dim(need, x * ny + y, 0, keepdims=False)
    my_rank = lax.dynamic_index_in_dim(rank, x * ny + y, 0, keepdims=False).astype(jnp.int32)
    row_need = lax.dynamic_index_in_dim(my_need.reshape(plane, nzh, halves), zh, 1, keepdims=False)
    row_rank = lax.dynamic_index_in_dim(my_rank.reshape(plane, nzh, halves), zh, 1, keepdims=False)
    row_rank = jnp.where(row_need, row_rank, -1).reshape(1, slices)
    pick = (row_rank == jnp.arange(LEVELS[-1], dtype=jnp.int32)[:, None]).astype(jnp.bfloat16)
    pick, my_rank = lax.optimization_barrier((pick, my_rank))

    def spread_y(piece):
        return jnp.broadcast_to(piece[None], (ny,) + piece.shape)

    def over_y(spread):
        return lax.all_to_all(spread, "y", 0, 0, tiled=True)

    cols, ready = lax.optimization_barrier((cols, spread_y(cols)))

    def attend(kept, operands):
        plane_rows, cols, ready, query, segment_ids, block_of_slot, value_up, my_rank, pick = operands
        few = kept < slices
        sent = plane_rows
        if few:
            sent = jnp.dot(pick[:kept], plane_rows, preferred_element_type=jnp.float32).astype(jnp.bfloat16)
        gathered = lax.all_gather(sent.reshape(kept * ROWS, LANES), ("zh", "zl", "core"), axis=0, tiled=True)
        gathered = gathered.reshape(-1, ROWS, LANES)

        cols, ready, sent = lax.optimization_barrier((cols, ready, sent))
        mine = over_y(ready)
        other = lax.ppermute(cols, "zh", [(i, nzh - 1 - i) for i in range(nzh)])
        theirs = over_y(spread_y(other))

        my_blocks, first, slot_of_block, lo_rows, q, vup = prepare(
            query, segment_ids, block_of_slot, value_up, seq_index
        )
        slot_seq, slot_half = slot_of_block // halves, slot_of_block % halves
        if few:
            slots = jnp.arange(block_of_slot.shape[0], dtype=jnp.int32)
            place = jnp.sum(jnp.where(slot_of_block[:, None] == slots[None, :], my_rank[None, :], 0), axis=1)
            place = jnp.minimum(place, kept - 1)
        else:
            place = slot_seq // nzh * halves + slot_half
        start = (slot_seq % nzh) * PARTS * kept + place
        scal = jnp.concatenate([my_blocks, first, start]).astype(jnp.int32)
        return attention(scal, lo_rows, q, vup, gathered, nx), mine, theirs

    head_values, mine, theirs = lax.switch(
        level,
        [functools.partial(attend, kept) for kept in (*LEVELS, slices)],
        (plane_rows, cols, ready, query, segment_ids, block_of_slot, value_up, my_rank, pick),
    )

    wide = head_values.shape[2]
    rows = lax.all_to_all(head_values, "x", 0, 0, tiled=True).reshape(nx, nc, toks // nc, wide)
    columns = jnp.where(zh == 0, jnp.stack([mine, theirs], 1), jnp.stack([theirs, mine], 1))
    columns = columns.reshape(-1, cols.shape[1])
    n_cols = columns.shape[0]
    own = toks // (nzl * nc)

    def project(which):
        part = lax.dynamic_index_in_dim(rows, which, 1, keepdims=False)
        return lax.dot_general(
            part.reshape(-1, wide), columns, (((1,), (1,)), ((), ())), preferred_element_type=jnp.float32
        )

    give = project(nc - 1 - core).astype(jnp.bfloat16)
    got = lax.ppermute(give, "core", [(i, nc - 1 - i) for i in range(nc)])
    keep = lax.optimization_barrier(project(core))
    chip = (keep + got.astype(jnp.float32)).astype(jnp.bfloat16)
    chip = chip.reshape(nx * nzl, own, n_cols)
    terms = lax.all_to_all(chip, ("x", "zl"), 0, 0, tiled=True)
    terms = terms.reshape(nx, nzl, own, n_cols)
    sums = [functools.reduce(jnp.add, [terms[i, j].astype(jnp.float32) for j in range(nzl)]) for i in range(nx)]
    return jnp.concatenate([each.astype(jnp.bfloat16) for each in sums], axis=1)


AXES = {"x": 4, "y": 8, "zh": 2, "zl": 4, "core": 2}


def solution(mesh):
    names = tuple(AXES)
    fine = Mesh(mesh.devices.reshape(tuple(AXES.values())), names)
    seq, head = names[:3], names[3:]
    return jax.shard_map(
        per_device,
        mesh=fine,
        in_specs=(
            P(seq, head, None),
            P(seq, None),
            P(),
            P(),
            P(head, None, None),
            P(head, seq),
        ),
        out_specs=P(names, None),
        check_vma=False,
    )
```

```python
import functools
import math

import jax
import jax.numpy as jnp
from jax import lax
from jax.experimental import pallas as pl
from jax.experimental.pallas import tpu as pltpu
from jax.sharding import Mesh
from jax.sharding import PartitionSpec as P

BLK = 64
CHUNK = 8
ROWS, LANES = 32, 128
PARTS = 8
OWN = 16
LEVELS = (40, 48)
exp2_scale = 192 ** (-0.5) * math.log2(math.e)
floor_max = -1e30
masked_score = -2e30


def attention_kernel(scal, lo_ref, q_ref, vup_ref, lat, out_ref, kbuf, acc, top, mass, done):
    heads, toks, width = q_ref.shape
    rows = heads * BLK
    slices = lat.shape[0] // 16
    across = width // LANES
    n_blocks = scal.shape[0] - 6

    def attend(b, base, size, masked):
        for j in range(size):
            src = scal[6 + jnp.minimum(base + j, n_blocks - 1)]
            for part in range(PARTS):
                row = j * BLK + part // across * ROWS
                lane = part % across * LANES
                kbuf[row : row + ROWS, lane : lane + LANES] = lat[src + part * slices]
        keys = kbuf[: size * BLK, :]
        q = q_ref[:, b * BLK : (b + 1) * BLK, :].reshape(rows, width)
        s = lax.dot_general(q, keys, (((1,), (1,)), ((), ())), preferred_element_type=jnp.float32)
        if masked:
            lo = lo_ref[:, b * BLK : (b + 1) * BLK, :].reshape(rows, 1)
            pos = scal[b] * BLK + lax.broadcasted_iota(jnp.int32, (heads, BLK, 1), 1).reshape(rows, 1)
            kp = base * BLK + lax.broadcasted_iota(jnp.int32, (1, size * BLK), 1)
            s = jnp.where((kp <= pos) & (kp >= lo), s, masked_score)
        tiles = [s[:, t : t + LANES] for t in range(0, size * BLK, LANES)]
        old = top[...]
        new = jnp.maximum(old, jnp.max(functools.reduce(jnp.maximum, tiles), axis=1, keepdims=True))
        factor = jnp.exp2((old - new) * exp2_scale)
        w = [jnp.exp2((tile - new) * exp2_scale) for tile in tiles]
        top[...] = new
        mass[...] = mass[...] * factor + functools.reduce(jnp.add, w)
        added = jnp.dot(
            jnp.concatenate([x.astype(jnp.bfloat16) for x in w], axis=1),
            keys,
            preferred_element_type=jnp.float32,
        )
        for t in range(across):
            lanes = slice(t * LANES, (t + 1) * LANES)
            acc[:, lanes] = acc[:, lanes] * factor + added[:, lanes]

    for b in range(toks // BLK):
        block, first, clean = scal[b], scal[2 + b], scal[4 + b]
        acc[...] = jnp.zeros_like(acc)
        top[...] = jnp.full_like(top, floor_max)
        mass[...] = jnp.zeros_like(mass)
        count = block - first + 1
        wide = (count + CHUNK - 1) // (2 * CHUNK)

        @pl.loop(0, wide)
        def _(i):
            base = first + i * 2 * CHUNK
            whole = (base >= clean) & (base + 2 * CHUNK <= block)

            @pl.when(whole)
            def _():
                attend(b, base, 2 * CHUNK, False)

            @pl.when(jnp.logical_not(whole))
            def _():
                attend(b, base, 2 * CHUNK, True)

        @pl.when(wide * 2 * CHUNK < count)
        def _():
            attend(b, first + wide * 2 * CHUNK, CHUNK, True)

        total = jnp.sum(mass[...], axis=1, keepdims=True)
        latent_out = (acc[...] / total).astype(jnp.bfloat16)
        done[:, b * BLK : (b + 1) * BLK, :] = latent_out.reshape(heads, BLK, width)

    vh = vup_ref.shape[2]
    for h in range(heads):
        values = jnp.dot(done[h], vup_ref[h], preferred_element_type=jnp.float32).astype(jnp.bfloat16)
        for copy in range(out_ref.shape[0]):
            for at in range(0, toks, OWN):
                to = (at // OWN % 2) * (toks // 2) + at // OWN // 2 * OWN
                out_ref[copy, to : to + OWN, h * vh : (h + 1) * vh] = values[at : at + OWN, :]


def attention(scal, lo, q, vup, lat, copies):
    heads, toks, width = q.shape
    vh = vup.shape[2]
    vmem = pl.BlockSpec(memory_space=pltpu.VMEM)
    return pl.pallas_call(
        attention_kernel,
        out_shape=jax.ShapeDtypeStruct((copies, toks, heads * vh), jnp.bfloat16),
        in_specs=[pl.BlockSpec(memory_space=pltpu.SMEM)] + [vmem] * 4,
        out_specs=vmem,
        scratch_shapes=[
            pltpu.VMEM((2 * CHUNK * BLK, width), jnp.bfloat16),
            pltpu.VMEM((heads * BLK, width), jnp.float32),
            pltpu.VMEM((heads * BLK, LANES), jnp.float32),
            pltpu.VMEM((heads * BLK, LANES), jnp.float32),
            pltpu.VMEM((heads, toks, width), jnp.bfloat16),
        ],
        compiler_params=pltpu.CompilerParams(vmem_limit_bytes=40 * 2**20),
        cost_estimate=pl.CostEstimate(
            flops=6 * 2**30, bytes_accessed=2 * lat.size, transcendentals=2**21
        ),
        name="latent_attention",
    )(scal, lo, q, vup, lat)


def prepare(query, segment_ids, block_of_slot, value_up, seq_index):
    toks, heads, _ = query.shape
    my_blocks = lax.dynamic_slice_in_dim(block_of_slot, 2 * seq_index, 2, 0)
    segs = jnp.concatenate(
        [lax.dynamic_slice_in_dim(segment_ids, my_blocks[i] * BLK, BLK, 0) for i in range(2)]
    )
    lo = jnp.sum((segment_ids[None, :] < segs[:, None]).astype(jnp.int32), axis=1)
    first = lo.reshape(2, BLK)[:, 0] // BLK
    clean = (lo.reshape(2, BLK)[:, BLK - 1] + BLK - 1) // BLK
    first = jnp.concatenate([first, clean])
    n = block_of_slot.shape[0]
    slots = jnp.arange(n, dtype=jnp.int32)
    slot_of_block = jnp.sum(
        jnp.where(block_of_slot[None, :] == slots[:, None], slots[None, :], 0), axis=1
    )
    lo_rows = jnp.broadcast_to(lo[None, :, None], (heads, toks, 1))
    q = query.transpose(1, 0, 2)
    vup = jnp.pad(value_up, ((0, 0), (0, query.shape[2] - value_up.shape[1]), (0, 0)))
    return my_blocks, first, slot_of_block, lo_rows, q, vup


def need_tables(segment_ids, block_of_slot, plane, nzh, halves):
    n = block_of_slot.shape[0]
    firsts = segment_ids.reshape(n, BLK)[:, 0]
    block_first = jnp.sum((segment_ids[None, :] < firsts[:, None]).astype(jnp.int32), axis=1) // BLK
    blocks = jnp.arange(n, dtype=jnp.int32)
    slot_first = jnp.sum(
        jnp.where(block_of_slot[:, None] == blocks[None, :], block_first[None, :], 0), axis=1
    )
    pair = (slot_first[:, None] <= block_of_slot[None, :]) & (
        block_of_slot[None, :] <= block_of_slot[:, None]
    )
    need = jnp.any(pair.reshape(plane, nzh * halves, n), axis=1)
    slot_plane = blocks // halves % nzh
    before = (blocks[:, None] < blocks[None, :]) & (slot_plane[:, None] == slot_plane[None, :])
    rank = jnp.dot(need.astype(jnp.bfloat16), before.astype(jnp.bfloat16), preferred_element_type=jnp.float32)
    most = jnp.max(jnp.where(need, rank, -1.0)) + 1.0
    level = sum((most > kept).astype(jnp.int32) for kept in LEVELS)
    return need, rank, level


def per_device(query, latent, segment_ids, block_of_slot, value_up, out_proj):
    nx, ny, nzh = (lax.axis_size(a) for a in ("x", "y", "zh"))
    nzl, nc = lax.axis_size("zl"), lax.axis_size("core")
    plane = nx * ny
    x, y, zh = (lax.axis_index(a) for a in ("x", "y", "zh"))
    zl, core = lax.axis_index("zl"), lax.axis_index("core")
    seq_index = (x * ny + y) * nzh + zh
    toks, width = latent.shape
    halves, across = toks // BLK, width // LANES
    slices = plane * halves

    cols = out_proj.T

    number = zl * nc + core
    corner = (0, number // across * ROWS, number % across * LANES)
    part = lax.dynamic_slice(latent.reshape(halves, BLK, width), corner, (halves, ROWS, LANES))
    line_rows = lax.all_to_all(jnp.broadcast_to(part[None], (ny,) + part.shape), "y", 0, 0, tiled=True)
    spread = jnp.broadcast_to(line_rows[None], (nx,) + line_rows.shape)
    plane_rows = lax.all_to_all(spread, "x", 0, 0, tiled=True)
    plane_rows = plane_rows.reshape(slices, ROWS * LANES)

    need, rank, level = need_tables(segment_ids, block_of_slot, plane, nzh, halves)
    my_need = lax.dynamic_index_in_dim(need, x * ny + y, 0, keepdims=False)
    my_rank = lax.dynamic_index_in_dim(rank, x * ny + y, 0, keepdims=False).astype(jnp.int32)
    row_need = lax.dynamic_index_in_dim(my_need.reshape(plane, nzh, halves), zh, 1, keepdims=False)
    row_rank = lax.dynamic_index_in_dim(my_rank.reshape(plane, nzh, halves), zh, 1, keepdims=False)
    row_rank = jnp.where(row_need, row_rank, -1).reshape(1, slices)
    pick = (row_rank == jnp.arange(LEVELS[-1], dtype=jnp.int32)[:, None]).astype(jnp.bfloat16)
    pick, my_rank = lax.optimization_barrier((pick, my_rank))

    def spread_y(piece):
        return jnp.broadcast_to(piece[None], (ny,) + piece.shape)

    def over_y(spread):
        return lax.all_to_all(spread, "y", 0, 0, tiled=True)

    cols, ready = lax.optimization_barrier((cols, spread_y(cols)))

    def attend(kept, operands):
        plane_rows, cols, ready, query, segment_ids, block_of_slot, value_up, my_rank, pick = operands
        few = kept < slices
        sent = plane_rows
        if few:
            sent = jnp.dot(pick[:kept], plane_rows, preferred_element_type=jnp.float32).astype(jnp.bfloat16)
        gathered = lax.all_gather(sent.reshape(kept * ROWS, LANES), ("zh", "zl", "core"), axis=0, tiled=True)
        gathered = gathered.reshape(-1, ROWS, LANES)

        cols, ready, sent = lax.optimization_barrier((cols, ready, sent))
        mine = over_y(ready)
        other = lax.ppermute(cols, "zh", [(i, nzh - 1 - i) for i in range(nzh)])
        theirs = over_y(spread_y(other))

        my_blocks, first, slot_of_block, lo_rows, q, vup = prepare(
            query, segment_ids, block_of_slot, value_up, seq_index
        )
        slot_seq, slot_half = slot_of_block // halves, slot_of_block % halves
        if few:
            slots = jnp.arange(block_of_slot.shape[0], dtype=jnp.int32)
            place = jnp.sum(jnp.where(slot_of_block[:, None] == slots[None, :], my_rank[None, :], 0), axis=1)
            place = jnp.minimum(place, kept - 1)
        else:
            place = slot_seq // nzh * halves + slot_half
        start = (slot_seq % nzh) * PARTS * kept + place
        scal = jnp.concatenate([my_blocks, first, start]).astype(jnp.int32)
        return attention(scal, lo_rows, q, vup, gathered, nx), mine, theirs

    head_values, mine, theirs = lax.switch(
        level,
        [functools.partial(attend, kept) for kept in (*LEVELS, slices)],
        (plane_rows, cols, ready, query, segment_ids, block_of_slot, value_up, my_rank, pick),
    )

    wide = head_values.shape[2]
    rows = lax.all_to_all(head_values, "x", 0, 0, tiled=True).reshape(nx, nc, toks // nc, wide)
    columns = jnp.where(zh == 0, jnp.stack([mine, theirs], 1), jnp.stack([theirs, mine], 1))
    columns = columns.reshape(-1, cols.shape[1])
    n_cols = columns.shape[0]
    own = toks // (nzl * nc)

    def project(which):
        part = lax.dynamic_index_in_dim(rows, which, 1, keepdims=False)
        return lax.dot_general(
            part.reshape(-1, wide), columns, (((1,), (1,)), ((), ())), preferred_element_type=jnp.float32
        )

    give = project(nc - 1 - core).astype(jnp.bfloat16)
    got = lax.ppermute(give, "core", [(i, nc - 1 - i) for i in range(nc)])
    keep = lax.optimization_barrier(project(core))
    chip = (keep + got.astype(jnp.float32)).astype(jnp.bfloat16)
    chip = chip.reshape(nx * nzl, own, n_cols)
    terms = lax.all_to_all(chip, ("x", "zl"), 0, 0, tiled=True)
    terms = terms.reshape(nx, nzl, own, n_cols)
    sums = [functools.reduce(jnp.add, [terms[i, j].astype(jnp.float32) for j in range(nzl)]) for i in range(nx)]
    return jnp.concatenate([each.astype(jnp.bfloat16) for each in sums], axis=1)


AXES = {"x": 4, "y": 8, "zh": 2, "zl": 4, "core": 2}


def solution(mesh):
    names = tuple(AXES)
    fine = Mesh(mesh.devices.reshape(tuple(AXES.values())), names)
    seq, head = names[:3], names[3:]
    return jax.shard_map(
        per_device,
        mesh=fine,
        in_specs=(
            P(seq, head, None),
            P(seq, None),
            P(),
            P(),
            P(head, None, None),
            P(head, seq),
        ),
        out_specs=P(names, None),
        check_vma=False,
    )
```

```python
import functools
import math

import jax
import jax.numpy as jnp
from jax import lax
from jax.experimental import pallas as pl
from jax.experimental.pallas import tpu as pltpu
from jax.sharding import Mesh
from jax.sharding import PartitionSpec as P

BLK = 64
CHUNK = 8
ROWS, LANES = 32, 128
PARTS = 8
OWN = 16
LEVELS = (40, 48)
exp2_scale = 192 ** (-0.5) * math.log2(math.e)
floor_max = -1e30
masked_score = -2e30


def attention_kernel(scal, lo_ref, q_ref, vup_ref, lat, out_ref, kbuf, acc, top, mass, done):
    heads, toks, width = q_ref.shape
    rows = heads * BLK
    slices = lat.shape[0] // 16
    across = width // LANES
    n_blocks = scal.shape[0] - 6

    def attend(b, base, size, masked):
        for j in range(size):
            src = scal[6 + jnp.minimum(base + j, n_blocks - 1)]
            for part in range(PARTS):
                row = j * BLK + part // across * ROWS
                lane = part % across * LANES
                kbuf[row : row + ROWS, lane : lane + LANES] = lat[src + part * slices]
        keys = kbuf[: size * BLK, :]
        q = q_ref[:, b * BLK : (b + 1) * BLK, :].reshape(rows, width)
        s = lax.dot_general(q, keys, (((1,), (1,)), ((), ())), preferred_element_type=jnp.float32)
        if masked:
            lo = lo_ref[:, b * BLK : (b + 1) * BLK, :].reshape(rows, 1)
            pos = scal[b] * BLK + lax.broadcasted_iota(jnp.int32, (heads, BLK, 1), 1).reshape(rows, 1)
            kp = base * BLK + lax.broadcasted_iota(jnp.int32, (1, size * BLK), 1)
            s = jnp.where((kp <= pos) & (kp >= lo), s, masked_score)
        tiles = [s[:, t : t + LANES] for t in range(0, size * BLK, LANES)]
        old = top[...]
        new = jnp.maximum(old, jnp.max(functools.reduce(jnp.maximum, tiles), axis=1, keepdims=True))
        factor = jnp.exp2((old - new) * exp2_scale)
        w = [jnp.exp2((tile - new) * exp2_scale) for tile in tiles]
        top[...] = new
        mass[...] = mass[...] * factor + functools.reduce(jnp.add, w)
        added = jnp.dot(
            jnp.concatenate([x.astype(jnp.bfloat16) for x in w], axis=1),
            keys,
            preferred_element_type=jnp.float32,
        )
        for t in range(across):
            lanes = slice(t * LANES, (t + 1) * LANES)
            acc[:, lanes] = acc[:, lanes] * factor + added[:, lanes]

    for b in range(toks // BLK):
        block, first, clean = scal[b], scal[2 + b], scal[4 + b]
        acc[...] = jnp.zeros_like(acc)
        top[...] = jnp.full_like(top, floor_max)
        mass[...] = jnp.zeros_like(mass)
        count = block - first + 1
        wide = (count + CHUNK - 1) // (2 * CHUNK)

        @pl.loop(0, wide)
        def _(i):
            base = first + i * 2 * CHUNK
            whole = (base >= clean) & (base + 2 * CHUNK <= block)

            @pl.when(whole)
            def _():
                attend(b, base, 2 * CHUNK, False)

            @pl.when(jnp.logical_not(whole))
            def _():
                attend(b, base, 2 * CHUNK, True)

        @pl.when(wide * 2 * CHUNK < count)
        def _():
            attend(b, first + wide * 2 * CHUNK, CHUNK, True)

        total = jnp.sum(mass[...], axis=1, keepdims=True)
        latent_out = (acc[...] / total).astype(jnp.bfloat16)
        done[:, b * BLK : (b + 1) * BLK, :] = latent_out.reshape(heads, BLK, width)

    vh = vup_ref.shape[2]
    for h in range(heads):
        values = jnp.dot(done[h], vup_ref[h], preferred_element_type=jnp.float32).astype(jnp.bfloat16)
        for copy in range(out_ref.shape[0]):
            for at in range(0, toks, OWN):
                to = (at // OWN % 2) * (toks // 2) + at // OWN // 2 * OWN
                out_ref[copy, to : to + OWN, h * vh : (h + 1) * vh] = values[at : at + OWN, :]


def attention(scal, lo, q, vup, lat, copies):
    heads, toks, width = q.shape
    vh = vup.shape[2]
    vmem = pl.BlockSpec(memory_space=pltpu.VMEM)
    return pl.pallas_call(
        attention_kernel,
        out_shape=jax.ShapeDtypeStruct((copies, toks, heads * vh), jnp.bfloat16),
        in_specs=[pl.BlockSpec(memory_space=pltpu.SMEM)] + [vmem] * 4,
        out_specs=vmem,
        scratch_shapes=[
            pltpu.VMEM((2 * CHUNK * BLK, width), jnp.bfloat16),
            pltpu.VMEM((heads * BLK, width), jnp.float32),
            pltpu.VMEM((heads * BLK, LANES), jnp.float32),
            pltpu.VMEM((heads * BLK, LANES), jnp.float32),
            pltpu.VMEM((heads, toks, width), jnp.bfloat16),
        ],
        compiler_params=pltpu.CompilerParams(vmem_limit_bytes=40 * 2**20),
        cost_estimate=pl.CostEstimate(
            flops=6 * 2**30, bytes_accessed=2 * lat.size, transcendentals=2**21
        ),
        name="latent_attention",
    )(scal, lo, q, vup, lat)


def prepare(query, segment_ids, block_of_slot, value_up, seq_index):
    toks, heads, _ = query.shape
    my_blocks = lax.dynamic_slice_in_dim(block_of_slot, 2 * seq_index, 2, 0)
    segs = jnp.concatenate(
        [lax.dynamic_slice_in_dim(segment_ids, my_blocks[i] * BLK, BLK, 0) for i in range(2)]
    )
    lo = jnp.sum((segment_ids[None, :] < segs[:, None]).astype(jnp.int32), axis=1)
    first = lo.reshape(2, BLK)[:, 0] // BLK
    clean = (lo.reshape(2, BLK)[:, BLK - 1] + BLK - 1) // BLK
    first = jnp.concatenate([first, clean])
    n = block_of_slot.shape[0]
    slots = jnp.arange(n, dtype=jnp.int32)
    slot_of_block = jnp.sum(
        jnp.where(block_of_slot[None, :] == slots[:, None], slots[None, :], 0), axis=1
    )
    lo_rows = jnp.broadcast_to(lo[None, :, None], (heads, toks, 1))
    q = query.transpose(1, 0, 2)
    vup = jnp.pad(value_up, ((0, 0), (0, query.shape[2] - value_up.shape[1]), (0, 0)))
    return my_blocks, first, slot_of_block, lo_rows, q, vup


def need_tables(segment_ids, block_of_slot, plane, nzh, halves):
    n = block_of_slot.shape[0]
    firsts = segment_ids.reshape(n, BLK)[:, 0]
    block_first = jnp.sum((segment_ids[None, :] < firsts[:, None]).astype(jnp.int32), axis=1) // BLK
    blocks = jnp.arange(n, dtype=jnp.int32)
    slot_first = jnp.sum(
        jnp.where(block_of_slot[:, None] == blocks[None, :], block_first[None, :], 0), axis=1
    )
    pair = (slot_first[:, None] <= block_of_slot[None, :]) & (
        block_of_slot[None, :] <= block_of_slot[:, None]
    )
    need = jnp.any(pair.reshape(plane, nzh * halves, n), axis=1)
    slot_plane = blocks // halves % nzh
    before = (blocks[:, None] < blocks[None, :]) & (slot_plane[:, None] == slot_plane[None, :])
    rank = jnp.dot(need.astype(jnp.bfloat16), before.astype(jnp.bfloat16), preferred_element_type=jnp.float32)
    most = jnp.max(jnp.where(need, rank, -1.0)) + 1.0
    level = sum((most > kept).astype(jnp.int32) for kept in LEVELS)
    return need, rank, level


def per_device(query, latent, segment_ids, block_of_slot, value_up, out_proj):
    nx, ny, nzh = (lax.axis_size(a) for a in ("x", "y", "zh"))
    nzl, nc = lax.axis_size("zl"), lax.axis_size("core")
    plane = nx * ny
    x, y, zh = (lax.axis_index(a) for a in ("x", "y", "zh"))
    zl, core = lax.axis_index("zl"), lax.axis_index("core")
    seq_index = (x * ny + y) * nzh + zh
    toks, width = latent.shape
    halves, across = toks // BLK, width // LANES
    slices = plane * halves

    cols = out_proj.T

    number = zl * nc + core
    corner = (0, number // across * ROWS, number % across * LANES)
    part = lax.dynamic_slice(latent.reshape(halves, BLK, width), corner, (halves, ROWS, LANES))
    spread = jnp.broadcast_to(part[None], (plane,) + part.shape)
    plane_rows = lax.all_to_all(spread, ("y", "x"), 0, 0, tiled=True)
    plane_rows = plane_rows.reshape(slices, ROWS * LANES)

    need, rank, level = need_tables(segment_ids, block_of_slot, plane, nzh, halves)
    my_need = lax.dynamic_index_in_dim(need, x * ny + y, 0, keepdims=False)
    my_rank = lax.dynamic_index_in_dim(rank, x * ny + y, 0, keepdims=False).astype(jnp.int32)
    row_rank = jnp.where(my_need, my_rank, -1).reshape(plane, nzh, halves)
    row_rank = lax.dynamic_index_in_dim(row_rank, zh, 1, keepdims=False)
    row_rank = row_rank.reshape(nx, ny, halves).transpose(1, 0, 2).reshape(1, slices)
    pick = (row_rank == jnp.arange(LEVELS[-1], dtype=jnp.int32)[:, None]).astype(jnp.bfloat16)
    pick, my_rank = lax.optimization_barrier((pick, my_rank))

    def spread_y(piece):
        return jnp.broadcast_to(piece[None], (ny,) + piece.shape)

    def over_y(spread):
        return lax.all_to_all(spread, "y", 0, 0, tiled=True)

    cols, ready = lax.optimization_barrier((cols, spread_y(cols)))

    def attend(kept, operands):
        plane_rows, cols, ready, query, segment_ids, block_of_slot, value_up, my_rank, pick = operands
        few = kept < slices
        sent = plane_rows
        if few:
            sent = jnp.dot(pick[:kept], plane_rows, preferred_element_type=jnp.float32).astype(jnp.bfloat16)
        gathered = lax.all_gather(sent.reshape(kept * ROWS, LANES), ("zh", "zl", "core"), axis=0, tiled=True)
        gathered = gathered.reshape(-1, ROWS, LANES)

        cols, ready, sent = lax.optimization_barrier((cols, ready, sent))
        mine = over_y(ready)
        other = lax.ppermute(cols, "zh", [(i, nzh - 1 - i) for i in range(nzh)])
        theirs = over_y(spread_y(other))

        my_blocks, first, slot_of_block, lo_rows, q, vup = prepare(
            query, segment_ids, block_of_slot, value_up, seq_index
        )
        slot_seq, slot_half = slot_of_block // halves, slot_of_block % halves
        if few:
            slots = jnp.arange(block_of_slot.shape[0], dtype=jnp.int32)
            place = jnp.sum(jnp.where(slot_of_block[:, None] == slots[None, :], my_rank[None, :], 0), axis=1)
            place = jnp.minimum(place, kept - 1)
        else:
            column = slot_seq // nzh
            place = (column % ny * nx + column // ny) * halves + slot_half
        start = (slot_seq % nzh) * PARTS * kept + place
        scal = jnp.concatenate([my_blocks, first, start]).astype(jnp.int32)
        return attention(scal, lo_rows, q, vup, gathered, nx), mine, theirs

    head_values, mine, theirs = lax.switch(
        level,
        [functools.partial(attend, kept) for kept in (*LEVELS, slices)],
        (plane_rows, cols, ready, query, segment_ids, block_of_slot, value_up, my_rank, pick),
    )

    wide = head_values.shape[2]
    rows = lax.all_to_all(head_values, "x", 0, 0, tiled=True).reshape(nx, nc, toks // nc, wide)
    columns = jnp.where(zh == 0, jnp.stack([mine, theirs], 1), jnp.stack([theirs, mine], 1))
    columns = columns.reshape(-1, cols.shape[1])
    n_cols = columns.shape[0]
    own = toks // (nzl * nc)

    def project(which):
        part = lax.dynamic_index_in_dim(rows, which, 1, keepdims=False)
        return lax.dot_general(
            part.reshape(-1, wide), columns, (((1,), (1,)), ((), ())), preferred_element_type=jnp.float32
        )

    give = project(nc - 1 - core).astype(jnp.bfloat16)
    got = lax.ppermute(give, "core", [(i, nc - 1 - i) for i in range(nc)])
    keep = lax.optimization_barrier(project(core))
    chip = (keep + got.astype(jnp.float32)).astype(jnp.bfloat16)
    chip = chip.reshape(nx * nzl, own, n_cols)
    terms = lax.all_to_all(chip, ("x", "zl"), 0, 0, tiled=True)
    terms = terms.reshape(nx, nzl, own, n_cols)
    sums = [functools.reduce(jnp.add, [terms[i, j].astype(jnp.float32) for j in range(nzl)]) for i in range(nx)]
    return jnp.concatenate([each.astype(jnp.bfloat16) for each in sums], axis=1)


AXES = {"x": 4, "y": 8, "zh": 2, "zl": 4, "core": 2}


def solution(mesh):
    names = tuple(AXES)
    fine = Mesh(mesh.devices.reshape(tuple(AXES.values())), names)
    seq, head = names[:3], names[3:]
    return jax.shard_map(
        per_device,
        mesh=fine,
        in_specs=(
            P(seq, head, None),
            P(seq, None),
            P(),
            P(),
            P(head, None, None),
            P(head, seq),
        ),
        out_specs=P(names, None),
        check_vma=False,
    )
```

```python
import functools
import math

import jax
import jax.numpy as jnp
from jax import lax
from jax.experimental import pallas as pl
from jax.experimental.pallas import tpu as pltpu
from jax.sharding import Mesh
from jax.sharding import PartitionSpec as P

BLK = 64
CHUNK = 8
ROWS, LANES = 32, 128
PARTS = 8
OWN = 16
LEVELS = (32, 36, 40, 48)
exp2_scale = 192 ** (-0.5) * math.log2(math.e)
floor_max = -1e30
masked_score = -2e30


def attention_kernel(scal, lo_ref, q_ref, vup_ref, lat, out_ref, kbuf, acc, top, mass, done):
    heads, toks, width = q_ref.shape
    rows = heads * BLK
    slices = lat.shape[0] // 16
    across = width // LANES
    n_blocks = scal.shape[0] - 6

    def attend(b, base, size, masked):
        for j in range(size):
            src = scal[6 + jnp.minimum(base + j, n_blocks - 1)]
            for part in range(PARTS):
                row = j * BLK + part // across * ROWS
                lane = part % across * LANES
                kbuf[row : row + ROWS, lane : lane + LANES] = lat[src + part * slices]
        keys = kbuf[: size * BLK, :]
        q = q_ref[:, b * BLK : (b + 1) * BLK, :].reshape(rows, width)
        s = lax.dot_general(q, keys, (((1,), (1,)), ((), ())), preferred_element_type=jnp.float32)
        if masked:
            lo = lo_ref[:, b * BLK : (b + 1) * BLK, :].reshape(rows, 1)
            pos = scal[b] * BLK + lax.broadcasted_iota(jnp.int32, (heads, BLK, 1), 1).reshape(rows, 1)
            kp = base * BLK + lax.broadcasted_iota(jnp.int32, (1, size * BLK), 1)
            s = jnp.where((kp <= pos) & (kp >= lo), s, masked_score)
        tiles = [s[:, t : t + LANES] for t in range(0, size * BLK, LANES)]
        old = top[...]
        new = jnp.maximum(old, jnp.max(functools.reduce(jnp.maximum, tiles), axis=1, keepdims=True))
        factor = jnp.exp2((old - new) * exp2_scale)
        w = [jnp.exp2((tile - new) * exp2_scale) for tile in tiles]
        top[...] = new
        mass[...] = mass[...] * factor + functools.reduce(jnp.add, w)
        added = jnp.dot(
            jnp.concatenate([x.astype(jnp.bfloat16) for x in w], axis=1),
            keys,
            preferred_element_type=jnp.float32,
        )
        for t in range(across):
            lanes = slice(t * LANES, (t + 1) * LANES)
            acc[:, lanes] = acc[:, lanes] * factor + added[:, lanes]

    for b in range(toks // BLK):
        block, first, clean = scal[b], scal[2 + b], scal[4 + b]
        acc[...] = jnp.zeros_like(acc)
        top[...] = jnp.full_like(top, floor_max)
        mass[...] = jnp.zeros_like(mass)
        count = block - first + 1
        wide = (count + CHUNK - 1) // (2 * CHUNK)

        @pl.loop(0, wide)
        def _(i):
            base = first + i * 2 * CHUNK
            whole = (base >= clean) & (base + 2 * CHUNK <= block)

            @pl.when(whole)
            def _():
                attend(b, base, 2 * CHUNK, False)

            @pl.when(jnp.logical_not(whole))
            def _():
                attend(b, base, 2 * CHUNK, True)

        @pl.when(wide * 2 * CHUNK < count)
        def _():
            attend(b, first + wide * 2 * CHUNK, CHUNK, True)

        total = jnp.sum(mass[...], axis=1, keepdims=True)
        latent_out = (acc[...] / total).astype(jnp.bfloat16)
        done[:, b * BLK : (b + 1) * BLK, :] = latent_out.reshape(heads, BLK, width)

    vh = vup_ref.shape[2]
    for h in range(heads):
        values = jnp.dot(done[h], vup_ref[h], preferred_element_type=jnp.float32).astype(jnp.bfloat16)
        for copy in range(out_ref.shape[0]):
            for at in range(0, toks, OWN):
                to = (at // OWN % 2) * (toks // 2) + at // OWN // 2 * OWN
                out_ref[copy, to : to + OWN, h * vh : (h + 1) * vh] = values[at : at + OWN, :]


def attention(scal, lo, q, vup, lat, copies):
    heads, toks, width = q.shape
    vh = vup.shape[2]
    vmem = pl.BlockSpec(memory_space=pltpu.VMEM)
    return pl.pallas_call(
        attention_kernel,
        out_shape=jax.ShapeDtypeStruct((copies, toks, heads * vh), jnp.bfloat16),
        in_specs=[pl.BlockSpec(memory_space=pltpu.SMEM)] + [vmem] * 4,
        out_specs=vmem,
        scratch_shapes=[
            pltpu.VMEM((2 * CHUNK * BLK, width), jnp.bfloat16),
            pltpu.VMEM((heads * BLK, width), jnp.float32),
            pltpu.VMEM((heads * BLK, LANES), jnp.float32),
            pltpu.VMEM((heads * BLK, LANES), jnp.float32),
            pltpu.VMEM((heads, toks, width), jnp.bfloat16),
        ],
        compiler_params=pltpu.CompilerParams(vmem_limit_bytes=40 * 2**20),
        cost_estimate=pl.CostEstimate(
            flops=6 * 2**30, bytes_accessed=2 * lat.size, transcendentals=2**21
        ),
        name="latent_attention",
    )(scal, lo, q, vup, lat)


def prepare(query, segment_ids, block_of_slot, value_up, seq_index):
    toks, heads, _ = query.shape
    my_blocks = lax.dynamic_slice_in_dim(block_of_slot, 2 * seq_index, 2, 0)
    segs = jnp.concatenate(
        [lax.dynamic_slice_in_dim(segment_ids, my_blocks[i] * BLK, BLK, 0) for i in range(2)]
    )
    lo = jnp.sum((segment_ids[None, :] < segs[:, None]).astype(jnp.int32), axis=1)
    first = lo.reshape(2, BLK)[:, 0] // BLK
    clean = (lo.reshape(2, BLK)[:, BLK - 1] + BLK - 1) // BLK
    first = jnp.concatenate([first, clean])
    n = block_of_slot.shape[0]
    slots = jnp.arange(n, dtype=jnp.int32)
    slot_of_block = jnp.sum(
        jnp.where(block_of_slot[None, :] == slots[:, None], slots[None, :], 0), axis=1
    )
    lo_rows = jnp.broadcast_to(lo[None, :, None], (heads, toks, 1))
    q = query.transpose(1, 0, 2)
    vup = jnp.pad(value_up, ((0, 0), (0, query.shape[2] - value_up.shape[1]), (0, 0)))
    return my_blocks, first, slot_of_block, lo_rows, q, vup


def need_tables(segment_ids, block_of_slot, plane, nzh, halves):
    n = block_of_slot.shape[0]
    firsts = segment_ids.reshape(n, BLK)[:, 0]
    block_first = jnp.sum((segment_ids[None, :] < firsts[:, None]).astype(jnp.int32), axis=1) // BLK
    blocks = jnp.arange(n, dtype=jnp.int32)
    slot_first = jnp.sum(
        jnp.where(block_of_slot[:, None] == blocks[None, :], block_first[None, :], 0), axis=1
    )
    pair = (slot_first[:, None] <= block_of_slot[None, :]) & (
        block_of_slot[None, :] <= block_of_slot[:, None]
    )
    need = jnp.any(pair.reshape(plane, nzh * halves, n), axis=1)
    slot_plane = blocks // halves % nzh
    before = (blocks[:, None] < blocks[None, :]) & (slot_plane[:, None] == slot_plane[None, :])
    rank = jnp.dot(need.astype(jnp.bfloat16), before.astype(jnp.bfloat16), preferred_element_type=jnp.float32)
    most = jnp.max(jnp.where(need, rank, -1.0)) + 1.0
    level = sum((most > kept).astype(jnp.int32) for kept in LEVELS)
    return need, rank, level


def per_device(query, latent, segment_ids, block_of_slot, value_up, out_proj):
    nx, ny, nzh = (lax.axis_size(a) for a in ("x", "y", "zh"))
    nzl, nc = lax.axis_size("zl"), lax.axis_size("core")
    plane = nx * ny
    x, y, zh = (lax.axis_index(a) for a in ("x", "y", "zh"))
    zl, core = lax.axis_index("zl"), lax.axis_index("core")
    seq_index = (x * ny + y) * nzh + zh
    toks, width = latent.shape
    halves, across = toks // BLK, width // LANES
    slices = plane * halves

    cols = out_proj.T

    number = zl * nc + core
    corner = (0, number // across * ROWS, number % across * LANES)
    part = lax.dynamic_slice(latent.reshape(halves, BLK, width), corner, (halves, ROWS, LANES))
    spread = jnp.broadcast_to(part[None], (plane,) + part.shape)
    plane_rows = lax.all_to_all(spread, ("x", "y"), 0, 0, tiled=True)
    plane_rows = plane_rows.reshape(slices, ROWS * LANES)

    need, rank, level = need_tables(segment_ids, block_of_slot, plane, nzh, halves)
    my_need = lax.dynamic_index_in_dim(need, x * ny + y, 0, keepdims=False)
    my_rank = lax.dynamic_index_in_dim(rank, x * ny + y, 0, keepdims=False).astype(jnp.int32)
    row_need = lax.dynamic_index_in_dim(my_need.reshape(plane, nzh, halves), zh, 1, keepdims=False)
    row_rank = lax.dynamic_index_in_dim(my_rank.reshape(plane, nzh, halves), zh, 1, keepdims=False)
    row_rank = jnp.where(row_need, row_rank, -1).reshape(1, slices)
    pick = (row_rank == jnp.arange(LEVELS[-1], dtype=jnp.int32)[:, None]).astype(jnp.bfloat16)
    pick, my_rank = lax.optimization_barrier((pick, my_rank))

    def spread_y(piece):
        return jnp.broadcast_to(piece[None], (ny,) + piece.shape)

    def over_y(spread):
        return lax.all_to_all(spread, "y", 0, 0, tiled=True)

    cols, ready = lax.optimization_barrier((cols, spread_y(cols)))

    def attend(kept, operands):
        plane_rows, cols, ready, query, segment_ids, block_of_slot, value_up, my_rank, pick = operands
        few = kept < slices
        sent = plane_rows
        if few:
            sent = jnp.dot(pick[:kept], plane_rows, preferred_element_type=jnp.float32).astype(jnp.bfloat16)
        gathered = lax.all_gather(sent.reshape(kept * ROWS, LANES), ("zh", "zl", "core"), axis=0, tiled=True)
        gathered = gathered.reshape(-1, ROWS, LANES)

        cols, ready, sent = lax.optimization_barrier((cols, ready, sent))
        mine = over_y(ready)
        other = lax.ppermute(cols, "zh", [(i, nzh - 1 - i) for i in range(nzh)])
        theirs = over_y(spread_y(other))

        my_blocks, first, slot_of_block, lo_rows, q, vup = prepare(
            query, segment_ids, block_of_slot, value_up, seq_index
        )
        slot_seq, slot_half = slot_of_block // halves, slot_of_block % halves
        if few:
            slots = jnp.arange(block_of_slot.shape[0], dtype=jnp.int32)
            place = jnp.sum(jnp.where(slot_of_block[:, None] == slots[None, :], my_rank[None, :], 0), axis=1)
            place = jnp.minimum(place, kept - 1)
        else:
            place = slot_seq // nzh * halves + slot_half
        start = (slot_seq % nzh) * PARTS * kept + place
        scal = jnp.concatenate([my_blocks, first, start]).astype(jnp.int32)
        return attention(scal, lo_rows, q, vup, gathered, nx), mine, theirs

    head_values, mine, theirs = lax.switch(
        level,
        [functools.partial(attend, kept) for kept in (*LEVELS, slices)],
        (plane_rows, cols, ready, query, segment_ids, block_of_slot, value_up, my_rank, pick),
    )

    wide = head_values.shape[2]
    rows = lax.all_to_all(head_values, "x", 0, 0, tiled=True).reshape(nx, nc, toks // nc, wide)
    columns = jnp.where(zh == 0, jnp.stack([mine, theirs], 1), jnp.stack([theirs, mine], 1))
    columns = columns.reshape(-1, cols.shape[1])
    n_cols = columns.shape[0]
    own = toks // (nzl * nc)

    def project(which):
        part = lax.dynamic_index_in_dim(rows, which, 1, keepdims=False)
        return lax.dot_general(
            part.reshape(-1, wide), columns, (((1,), (1,)), ((), ())), preferred_element_type=jnp.float32
        )

    give = project(nc - 1 - core).astype(jnp.bfloat16)
    got = lax.ppermute(give, "core", [(i, nc - 1 - i) for i in range(nc)])
    keep = lax.optimization_barrier(project(core))
    chip = (keep + got.astype(jnp.float32)).astype(jnp.bfloat16)
    chip = chip.reshape(nx * nzl, own, n_cols)
    terms = lax.all_to_all(chip, ("x", "zl"), 0, 0, tiled=True)
    terms = terms.reshape(nx, nzl, own, n_cols)
    sums = [functools.reduce(jnp.add, [terms[i, j].astype(jnp.float32) for j in range(nzl)]) for i in range(nx)]
    return jnp.concatenate([each.astype(jnp.bfloat16) for each in sums], axis=1)


AXES = {"x": 4, "y": 8, "zh": 2, "zl": 4, "core": 2}


def solution(mesh):
    names = tuple(AXES)
    fine = Mesh(mesh.devices.reshape(tuple(AXES.values())), names)
    seq, head = names[:3], names[3:]
    return jax.shard_map(
        per_device,
        mesh=fine,
        in_specs=(
            P(seq, head, None),
            P(seq, None),
            P(),
            P(),
            P(head, None, None),
            P(head, seq),
        ),
        out_specs=P(names, None),
        check_vma=False,
    )
```
